512 devices in a mesh: row: 32 (over z_hi, x, core), col: 16 (over z_lo, y).
Axes of the slice: x: 4, y: 4, z: 16 (z_hi: 4, z_lo: 4; z = z_hi * 4 + z_lo), core: 2. Of those that a mesh axis runs over, the one named last changes fastest.
Arguments:
- matrix: float32 [16384, 16384], P('row', 'col'), may hold values from -40 to 40
Outputs:
- rotated: float32 [16384, 16384], P('row', 'col')
The draws below stay inside these ranges and needn't reach their ends.
All inputs are finite; a program needn't handle non-finite values.
Results may differ from the reference program's by a relative error of at most 0.0003.
Values sent between devices are 32-bit elements; how exact they have to be, the bound alone decides.
A program may use at most 64 MiB of HBM per device.

```python
import math
import jax
import jax.numpy as jnp
import numpy as np
from jax import lax

BLK = 128
INNER = 4
NEWTON = 2
NMAT = 16384


def draw_matrix(key, part):
    key = jax.random.fold_in(key, 11)
    first_key = jax.random.fold_in(key, 0)
    entries = jnp.clip(jax.random.normal(first_key, (NMAT, NMAT), jnp.float32), -6.0, 6.0)
    sym = (entries + entries.T) * (1.0 / math.sqrt(2.0))
    return sym.astype(jnp.float32)


def setup_inputs(seed: int = 0) -> dict:
    keys = jax.random.split(jax.random.key(seed), 2)
    matrix = draw_matrix(jax.random.fold_in(keys[1], 71), 0)
    return {"matrix": matrix}


def product(first, second):
    return jnp.dot(first, second, precision=lax.Precision.HIGHEST, preferred_element_type=jnp.float32)

def pair_rotation(square):
    order_size = square.shape[0]
    weights = jnp.arange(order_size, dtype=jnp.float32) / (order_size - 1) - 0.5
    stride = 0.25 / math.sqrt(order_size)
    identity = jnp.eye(order_size, dtype=jnp.float32)
    current = square
    rotation = identity
    for inner_step in range(INNER):
        bracket = current * weights[None, :] - weights[:, None] * current
        factor = identity + stride * bracket
        for polish in range(NEWTON):
            factor = 1.5 * factor - 0.5 * product(factor, product(factor.T, factor))
        current = product(factor.T, product(current, factor))
        rotation = product(rotation, factor)
    return rotation

def source_blocks(pair_count):
    source = np.zeros(2 * pair_count, np.int32)
    source[0] = 0
    source[2] = 1
    for k in range(2, pair_count):
        source[2 * k] = 2 * (k - 1)
    for k in range(pair_count - 1):
        source[2 * k + 1] = 2 * (k + 1) + 1
    source[2 * pair_count - 1] = 2 * (pair_count - 1)
    return source

def reference(matrix):
    pair_size = 2 * BLK
    pair_count = NMAT // pair_size

    def solve_one(index):
        offset_rows = (index * pair_size).astype(jnp.int32)
        square = lax.dynamic_slice(matrix, (offset_rows, offset_rows), (pair_size, pair_size))
        return pair_rotation(square)
    rotations = lax.map(solve_one, jnp.arange(pair_count, dtype=jnp.int32))
    rotated_rows = jnp.einsum('kpq,kpn->kqn', rotations, matrix.reshape(pair_count, pair_size, NMAT), precision=lax.Precision.HIGHEST).reshape(NMAT, NMAT)
    turned = jnp.einsum('mkp,kpq->mkq', rotated_rows.reshape(NMAT, pair_count, pair_size), rotations, precision=lax.Precision.HIGHEST).reshape(NMAT, NMAT)
    source = source_blocks(pair_count)
    blocks = turned.reshape(2 * pair_count, BLK, 2 * pair_count, BLK)
    blocks = blocks[source][:, :, source]
    return blocks.reshape(NMAT, NMAT)
```

```python
import math

import jax
import jax.numpy as jnp
from jax import lax
from jax.experimental import pallas as pl
from jax.experimental.pallas import tpu as pltpu
from jax.sharding import PartitionSpec as P

MESH = pl.DeviceIdType.MESH
F32 = jnp.float32
BF16 = jnp.bfloat16
BLK = 128
PAIR = 256
INNER = 4
ROWS = 512
COLS = 1024
WIDE = COLS + 2 * PAIR
GROUPS = 16
FOLD = 264


def split(value):
    high = value.astype(BF16)
    return high, (value - high.astype(F32)).astype(BF16)


def product(first, second):
    (first_high, first_low), (second_high, second_low) = first, second
    left = jnp.concatenate([first_high, first_high, first_low], axis=1)
    right = jnp.concatenate([second_high, second_low, second_high], axis=0)
    return jnp.dot(left, right, preferred_element_type=F32)


def pair_rotation(square):
    i = lax.broadcasted_iota(jnp.int32, (PAIR, PAIR), 0)
    j = lax.broadcasted_iota(jnp.int32, (PAIR, PAIR), 1)
    weights = (j - i).astype(F32) * (0.25 / math.sqrt(PAIR) / (PAIR - 1))
    identity = jnp.where(i == j, 1.0, 0.0).astype(F32)
    current = square
    rotation = None
    for inner_step in range(INNER):
        last = inner_step == INNER - 1
        bracket = current * weights
        bracket_s = split(bracket)
        power = product(bracket_s, bracket_s)
        power_s = split(power)
        if not last:
            half = current + product(split(current), bracket_s)
        if rotation is None:
            turned = identity + bracket
        else:
            turned = rotation + product(split(rotation), bracket_s)
        power2 = product(power_s, power_s)
        if not last:
            both = half - product(bracket_s, split(half))
        series = 0.375 * identity + 0.3125 * power + 0.0625 * power2
        polish = split(0.5 * power + product(split(power2), split(series)))
        rotation = turned + product(split(turned), polish)
        if not last:
            half = both + product(split(both), polish)
            current = half + product(polish, split(half))
    return rotation


def fold(square):
    i = lax.broadcasted_iota(jnp.int32, (BLK, BLK), 0)
    j = lax.broadcasted_iota(jnp.int32, (BLK, BLK), 1)
    first, second = square[:BLK, :BLK], square[BLK:, BLK:]
    diagonal = jnp.sum(jnp.where(i == j, second, 0.0), axis=0, keepdims=True)
    return jnp.concatenate(
        [square[:BLK, BLK:], jnp.where(i <= j, first, second), jnp.broadcast_to(diagonal, (8, BLK))], axis=0
    )


def unfold(folded):
    i = lax.broadcasted_iota(jnp.int32, (BLK, BLK), 0)
    j = lax.broadcasted_iota(jnp.int32, (BLK, BLK), 1)
    side = folded[:BLK]
    middle = folded[BLK : 2 * BLK]
    flipped = middle.T
    first = jnp.where(i <= j, middle, flipped)
    second = jnp.where(i > j, middle, jnp.where(i < j, flipped, folded[2 * BLK : 2 * BLK + 1]))
    return jnp.concatenate(
        [jnp.concatenate([first, side], axis=1), jnp.concatenate([side.T, second], axis=1)], axis=0
    )


def choose(cond, yes, no):
    return cond * yes + (1 - cond) * no


def same(a, b):
    return int(a == b) if isinstance(a - b, int) else jnp.where(a == b, 1, 0)


def slot_of(group, member, half):
    step, slot = 0, 0
    for m, h, slot_in, step_in in (
        (0, 0, 2, 0), (1, 0, 4, 0), (2, 0, 6, 0), (3, 0, 0, 1),
        (0, 1, 7, -1), (1, 1, 1, 0), (2, 1, 3, 0), (3, 1, 5, 0),
    ):
        if h == half:
            slot = slot + same(member, m) * slot_in
            step = step + same(member, m) * step_in
    first, last = same(group, 0), same(group, GROUPS - 1)
    if half == 0:
        slot = slot - first * same(member, 0) * 2 + last * same(member, 3) * 7
        step = step - last * same(member, 3)
    else:
        slot = slot - first * same(member, 0) * 5
        step = step + first * same(member, 0)
    return step, slot


def maker_of(group, slot):
    step, member = {0: (-1, 3), 1: (0, 1), 2: (0, 0), 3: (0, 2), 4: (0, 1), 5: (0, 3), 6: (0, 2), 7: (1, 0)}[slot]
    if slot == 0:
        return choose(same(group, 0), 0, step), choose(same(group, 0), 0, member)
    if slot == 7:
        return choose(same(group, GROUPS - 1), 0, step), choose(same(group, GROUPS - 1), 3, member)
    return step, member


class Place:
    def __init__(self, row, col):
        self.row, self.c = row, col
        self.k, self.R = row % 2, row // 2
        self.x, self.zh = self.R % 4, self.R // 4
        self.y, self.zl = self.c % 4, self.c // 4
        self.on_diagonal = same(self.R, self.c)
        self.in_relay = same(self.zh, self.zl)
        self.turn = (self.zh - self.zl + 4) % 4

    def at(self, k=None, x=None, zh=None, y=None, zl=None):
        k = self.k if k is None else k
        x = self.x if x is None else x
        zh = self.zh if zh is None else zh
        y = self.y if y is None else y
        zl = self.zl if zl is None else zl
        return (2 * (4 * zh + x) + k, 4 * zl + y)


def scatter_out(p):
    found = []
    for j in range(2):
        q = 2 * p.k + j
        own = (1 - p.k) * same(p.x, q)
        found.append((j, "col", p.on_diagonal * own, p.on_diagonal * (1 - own), p.at(k=0, x=q)))
        own = p.k * same(p.y, q)
        found.append((j, "row", p.on_diagonal * own, p.on_diagonal * (1 - own), p.at(k=1, y=q)))
    return found


def cross_out(p):
    col = 1 - p.k
    up, down = p.at(zh=(p.zh + 1) % 4), p.at(zh=(p.zh + 3) % 4)
    found = [
        (col * same(p.turn, 0), up, 0),
        (col * same(p.turn, 0), down, 0),
        (col * same(p.turn, 1), up, 1),
        (col * same(p.turn, 3), down, 2),
    ]
    for t in range(1, 4):
        found.append((p.k * p.in_relay, p.at(zl=(p.zl + t) % 4), 0))
    return found


def spread_out(p):
    found = []
    for half in range(2):
        step, slot = slot_of(p.c, p.x, half)
        core = slot % 2
        for t in (2, 1, 3, 0):
            own = (same(step, 0) * (1 - core)) if t == 0 else 0
            device = (2 * (4 * p.zh + (p.x + t) % 4) + core, p.c + step)
            found.append(("col", half, (1 - p.k) * own, (1 - p.k) * (1 - own), device, slot))
        step, slot = slot_of(p.R, p.y, half)
        core = slot // 4
        for t in (2, 1, 3, 0):
            own = (same(step, 0) * core) if t == 0 else 0
            device = (2 * (p.R + step) + core, 4 * p.zl + (p.y + t) % 4)
            found.append(("row", half, p.k * own, p.k * (1 - own), device, slot % 4))
    return found


def outer_out(p):
    forward = p.k
    here = choose(forward, 1 - same(p.R, GROUPS - 1), 1 - same(p.R, 0))
    edge = choose(forward, same(p.x, 3), same(p.x, 0))
    far_x = choose(forward, 0, 3)
    to_zh = (p.zh + choose(forward, 1, 3)) % 4
    next_row = (2 * (p.R + 2 * forward - 1) + 1 - p.k + 32) % 32
    found = []
    for q in range(4):
        relayed = here * edge * (1 - same(far_x, q))
        row = choose(edge, 2 * (4 * to_zh + q) + 1 - p.k, next_row)
        found.append((q, relayed, here * (1 - relayed), (row, p.c)))
    return found


def relay_role(p):
    forward = 1 - p.k
    far_x = choose(forward, 0, 3)
    near_x = choose(forward, 3, 0)
    inside = choose(forward, 1 - same(p.zh, 0), 1 - same(p.zh, 3))
    cond = inside * (1 - same(p.x, far_x))
    from_zh = (p.zh + choose(forward, 3, 1)) % 4
    return cond, p.at(x=far_x), p.at(k=1 - p.k, x=near_x, zh=from_zh)


def edges_out(p):
    found = [(cond, device) for _, _, _, cond, device in scatter_out(p)]
    found += [(cond, device) for cond, device, _ in cross_out(p)]
    found += [(cond, device) for _, _, _, cond, device, _ in spread_out(p)]
    for _, relayed, direct, device in outer_out(p):
        found.append((relayed + direct, device))
    cond, device, _ = relay_role(p)
    found.append((cond, device))
    found.append((1, p.at(k=1 - p.k)))
    found.append((1 - same(p.c, 0), (p.row, p.c - 1)))
    found.append((1 - same(p.c, GROUPS - 1), (p.row, p.c + 1)))
    return found


def edges_in(p):
    col = 1 - p.k
    source = p.at(k=p.x // 2, x=p.y)
    found = [(col * p.in_relay * (1 - same(p.x, p.y) * (1 - p.x // 2)), source)]
    source = p.at(k=p.y // 2, y=p.x)
    found.append((p.k * p.in_relay * (1 - same(p.x, p.y) * (p.y // 2)), source))
    up, down = p.at(zh=(p.zh + 1) % 4), p.at(zh=(p.zh + 3) % 4)
    found.append((col * (same(p.turn, 1) + same(p.turn, 2)), down))
    found.append((col * (same(p.turn, 3) + same(p.turn, 2)), up))
    found.append((p.k * (1 - p.in_relay), p.at(zl=p.zh)))
    for n in range(4):
        step, member = maker_of(p.c, 2 * n)
        step1, member1 = maker_of(p.c, 2 * n + 1)
        step, member = choose(p.k, step1, step), choose(p.k, member1, member)
        own = same(step, 0) * same(member, p.x) * (1 - p.k)
        found.append((1 - own, (2 * (4 * p.zh + member), p.c + step)))
        step, member = maker_of(p.R, n)
        step1, member1 = maker_of(p.R, 4 + n)
        step, member = choose(p.k, step1, step), choose(p.k, member1, member)
        own = same(step, 0) * same(member, p.y) * p.k
        found.append((1 - own, (2 * (p.R + step) + 1, 4 * p.zl + member)))
    forward = 1 - p.k
    here = choose(forward, 1 - same(p.R, 0), 1 - same(p.R, GROUPS - 1))
    far_x = choose(forward, 0, 3)
    edge = same(p.x, far_x)
    relay, _, start = relay_role(p)
    source_row = (2 * (p.R + 1 - 2 * forward) + 1 - p.k + 32) % 32
    for q in range(4):
        direct = choose(edge, same(far_x, q), 1)
        row = choose(edge, choose(direct, start[0], p.at(x=q)[0]), source_row)
        found.append((here, (row, p.c)))
    found.append((relay, start))
    found.append((1, p.at(k=1 - p.k)))
    found.append((1 - same(p.c, 0), (p.row, p.c - 1)))
    found.append((1 - same(p.c, GROUPS - 1), (p.row, p.c + 1)))
    return found


def here():
    return Place(lax.axis_index("row"), lax.axis_index("col"))


def when(cond, action):
    if isinstance(cond, int):
        if cond:
            action()
    else:
        pl.when(cond == 1)(action)


class Sends:
    def __init__(self, sems):
        self.sems, self.pending = sems, []

    def start(self, cond, source, target, recv_sem, device):
        index = len(self.pending)

        def make():
            return pltpu.make_async_remote_copy(
                src_ref=source,
                dst_ref=target,
                send_sem=self.sems.at[index],
                recv_sem=recv_sem,
                device_id=device,
                device_id_type=MESH,
            )

        self.pending.append((cond, make))
        when(cond, lambda: make().start())

    def finish(self):
        for cond, make in self.pending:
            when(cond, lambda make=make: make().wait_send())


def arrived(ref, sem, cond=1):
    when(cond, lambda: pltpu.make_async_copy(ref, ref, sem).wait())


def travel_kernel(
    m_ref, left_ref, right_ref, outer_ref, inner_ref, jc_ref, jr_ref,
    square, folded, solver_in, out_c, out_r, relay,
    load_sem, send_sem, solver_sem, jc_sem, jr_sem, side_sem, outer_sem, outer_side_sem, inner_sem, relay_sem,
):
    p = here()
    loads = []
    for j in range(2):
        column = pl.multiple_of(p.k * ROWS + j * PAIR, PAIR)
        loads.append(
            pltpu.make_async_copy(
                m_ref.at[pl.ds(j * PAIR, PAIR), pl.ds(column, PAIR)], square.at[j], load_sem.at[j]
            )
        )
        when(p.on_diagonal, loads[j].start)

    barrier = pltpu.get_barrier_semaphore()
    for cond, device in edges_in(p):
        when(
            cond,
            lambda device=device: pl.semaphore_signal(barrier, inc=1, device_id=device, device_id_type=MESH),
        )

    def fold_both():
        for j in range(2):
            loads[j].wait()
            folded[j] = fold(square[j])

    when(p.on_diagonal, fold_both)
    pl.semaphore_wait(barrier, sum(cond for cond, _ in edges_out(p)))

    sends = Sends(send_sem)
    mate = p.at(k=1 - p.k)
    before, after = (p.row, p.c - 1), (p.row, p.c + 1)
    has_before, has_after = 1 - same(p.c, 0), 1 - same(p.c, GROUPS - 1)
    low = pl.multiple_of(p.k * PAIR, PAIR)
    other = pl.multiple_of((1 - p.k) * PAIR, PAIR)

    for j, _, own, cond, device in scatter_out(p):
        sends.start(cond, folded.at[j], solver_in, solver_sem.at[0], device)
        when(own, pltpu.make_async_copy(folded.at[j], solver_in, solver_sem.at[0]).start)

    sends.start(has_before, m_ref.at[:, pl.ds(0, PAIR)], right_ref, side_sem.at[1], before)
    sends.start(has_after, m_ref.at[:, pl.ds(COLS - PAIR, PAIR)], left_ref, side_sem.at[0], after)
    sends.start(1, m_ref.at[pl.ds(other, PAIR)], inner_ref.at[:, pl.ds(PAIR, COLS)], inner_sem.at[0], mate)
    for q, relayed, direct, device in outer_out(p):
        part = m_ref.at[pl.ds(low, PAIR), pl.ds(q * PAIR, PAIR)]
        sends.start(relayed, part, relay, relay_sem.at[0], device)
        sends.start(direct, part, outer_ref.at[:, pl.ds(PAIR + q * PAIR, PAIR)], outer_sem.at[q], device)

    whole = choose(1 - p.k, 1 - same(p.turn, 2), 1)
    halves = 1 - whole
    parts = (pl.ds(0, BLK), pl.ds(BLK, FOLD - BLK))
    arrived(solver_in, solver_sem.at[0], whole)
    for n in range(2):
        arrived(solver_in.at[parts[n]], solver_sem.at[1 + n], halves)
    for cond, device, part in cross_out(p):
        ref = solver_in if part == 0 else solver_in.at[parts[part - 1]]
        sends.start(cond, ref, ref, solver_sem.at[part], device)

    rotation = pair_rotation(unfold(solver_in[...]))

    def keep_columns():
        for half in range(2):
            out_c[half] = rotation[:, half * BLK : (half + 1) * BLK]

    def keep_rows():
        flipped = rotation.T
        for half in range(2):
            out_r[half] = flipped[half * BLK : (half + 1) * BLK]

    when(1 - p.k, keep_columns)
    when(p.k, keep_rows)
    for kind, half, own, cond, device, slot in spread_out(p):
        source, target, sem = (out_c, jc_ref, jc_sem) if kind == "col" else (out_r, jr_ref, jr_sem)
        sends.start(cond, source.at[half], target.at[slot], sem.at[slot], device)
        if not isinstance(own, int) or own:
            when(own, pltpu.make_async_copy(source.at[half], target.at[slot], sem.at[slot]).start)

    relaying, relay_to, relay_from = relay_role(p)
    arrived(relay, relay_sem.at[0], relaying)
    sends.start(
        relaying, relay, outer_ref.at[:, pl.ds(pl.multiple_of(PAIR + p.x * PAIR, PAIR), PAIR)], outer_sem.at[p.x], relay_to
    )

    arrived(left_ref, side_sem.at[0], has_before)
    sends.start(has_before, left_ref.at[pl.ds(other, PAIR)], inner_ref.at[:, pl.ds(0, PAIR)], inner_sem.at[1], mate)
    arrived(right_ref, side_sem.at[1], has_after)
    sends.start(
        has_after, right_ref.at[pl.ds(other, PAIR)], inner_ref.at[:, pl.ds(PAIR + COLS, PAIR)], inner_sem.at[2], mate
    )
    has_outer = choose(p.k, 1 - same(p.R, GROUPS - 1), 1 - same(p.R, 0))
    for q in range(4):
        arrived(outer_ref.at[:, pl.ds(PAIR + q * PAIR, PAIR)], outer_sem.at[q], has_outer)
        if q == 0:
            sends.start(
                has_outer * has_before, outer_ref.at[:, pl.ds(PAIR, PAIR)], outer_ref.at[:, pl.ds(PAIR + COLS, PAIR)],
                outer_side_sem.at[1], before,
            )
    sends.start(
        has_outer * has_after, outer_ref.at[:, pl.ds(COLS, PAIR)], outer_ref.at[:, pl.ds(0, PAIR)],
        outer_side_sem.at[0], after,
    )

    for n in range(4):
        slot = 2 * n + p.k
        arrived(jc_ref.at[slot], jc_sem.at[slot])
        sends.start(1, jc_ref.at[slot], jc_ref.at[slot], jc_sem.at[slot], mate)
    for n in range(4):
        arrived(jc_ref.at[2 * n + 1 - p.k], jc_sem.at[2 * n + 1 - p.k])
        arrived(jr_ref.at[n], jr_sem.at[n])

    arrived(inner_ref.at[:, pl.ds(PAIR, COLS)], inner_sem.at[0])
    arrived(inner_ref.at[:, pl.ds(0, PAIR)], inner_sem.at[1], has_before)
    arrived(inner_ref.at[:, pl.ds(PAIR + COLS, PAIR)], inner_sem.at[2], has_after)
    arrived(outer_ref.at[:, pl.ds(0, PAIR)], outer_side_sem.at[0], has_outer * has_before)
    arrived(outer_ref.at[:, pl.ds(PAIR + COLS, PAIR)], outer_side_sem.at[1], has_outer * has_after)
    sends.finish()


def travel(matrix):
    any_spec = pl.BlockSpec(memory_space=pl.ANY)
    shapes = [(ROWS, PAIR), (ROWS, PAIR), (PAIR, WIDE), (PAIR, WIDE), (8, PAIR, BLK), (4, BLK, PAIR)]
    return pl.pallas_call(
        travel_kernel,
        out_shape=[jax.ShapeDtypeStruct(shape, F32) for shape in shapes],
        in_specs=[any_spec],
        out_specs=[any_spec] * len(shapes),
        scratch_shapes=[
            pltpu.VMEM((2, PAIR, PAIR), F32),
            pltpu.VMEM((2, FOLD, BLK), F32),
            pltpu.VMEM((FOLD, BLK), F32),
            pltpu.VMEM((2, PAIR, BLK), F32),
            pltpu.VMEM((2, BLK, PAIR), F32),
            pltpu.VMEM((PAIR, PAIR), F32),
            pltpu.SemaphoreType.DMA((2,)),
            pltpu.SemaphoreType.DMA((64,)),
            pltpu.SemaphoreType.DMA((3,)),
            pltpu.SemaphoreType.DMA((8,)),
            pltpu.SemaphoreType.DMA((4,)),
            pltpu.SemaphoreType.DMA((2,)),
            pltpu.SemaphoreType.DMA((4,)),
            pltpu.SemaphoreType.DMA((2,)),
            pltpu.SemaphoreType.DMA((3,)),
            pltpu.SemaphoreType.DMA((1,)),
        ],
        compiler_params=pltpu.CompilerParams(
            collective_id=1, has_side_effects=True, vmem_limit_bytes=32 * 1024 * 1024
        ),
        cost_estimate=pl.CostEstimate(flops=10**9, bytes_accessed=10**7, transcendentals=0),
        name="travel",
    )(matrix)


SLOTS = (((0,), 0), ((1, 4), 2), ((2,), 1), ((3, 6), 3), ((5,), 4), ((7,), 5))


def apply_kernel(
    m_ref, left_ref, right_ref, outer_ref, inner_ref, jc_ref, jr_ref, o_ref, raw, jc, jr, half_high, half_low, result,
    raw_sem, j_sem, out_sem,
):
    p = here()
    first_col, last_col = same(p.c, 0), same(p.c, GROUPS - 1)
    first_row, last_row = same(p.row, 0), same(p.row, 2 * GROUPS - 1)
    copies_j = [
        pltpu.make_async_copy(jr_ref, jr, j_sem.at[0]),
        pltpu.make_async_copy(jc_ref, jc, j_sem.at[1]),
    ]
    for copy in copies_j:
        copy.start()
    low, middle, high = pl.ds(0, PAIR), pl.ds(PAIR, COLS), pl.ds(PAIR + COLS, PAIR)

    def own_rows(s, pair, cond):
        rows = pl.ds(pair * PAIR, PAIR)
        when(cond, pltpu.make_async_copy(m_ref.at[rows], raw.at[s, :, middle], raw_sem.at[s, 0]).start)
        when(cond * (1 - first_col), pltpu.make_async_copy(left_ref.at[rows], raw.at[s, :, low], raw_sem.at[s, 1]).start)
        when(cond * (1 - last_col), pltpu.make_async_copy(right_ref.at[rows], raw.at[s, :, high], raw_sem.at[s, 2]).start)
        when(
            cond * first_col,
            pltpu.make_async_copy(m_ref.at[rows, pl.ds(0, PAIR)], raw.at[s, :, low], raw_sem.at[s, 1]).start,
        )
        when(
            cond * last_col,
            pltpu.make_async_copy(m_ref.at[rows, pl.ds(COLS - PAIR, PAIR)], raw.at[s, :, high], raw_sem.at[s, 2]).start,
        )

    def sent_rows(s, ref, cond):
        when(cond, pltpu.make_async_copy(ref.at[:, middle], raw.at[s, :, middle], raw_sem.at[s, 0]).start)
        when(cond * (1 - first_col), pltpu.make_async_copy(ref.at[:, low], raw.at[s, :, low], raw_sem.at[s, 1]).start)
        when(cond * (1 - last_col), pltpu.make_async_copy(ref.at[:, high], raw.at[s, :, high], raw_sem.at[s, 2]).start)
        when(
            cond * first_col,
            pltpu.make_async_copy(ref.at[:, pl.ds(PAIR, PAIR)], raw.at[s, :, low], raw_sem.at[s, 1]).start,
        )
        when(
            cond * last_col,
            pltpu.make_async_copy(ref.at[:, pl.ds(COLS, PAIR)], raw.at[s, :, high], raw_sem.at[s, 2]).start,
        )

    own_rows(1, 1, 1)
    own_rows(2, 0, 1)
    own_rows(0, 0, first_row)
    sent_rows(0, outer_ref, (1 - p.k) * (1 - first_row))
    sent_rows(0, inner_ref, p.k)
    own_rows(3, 1, last_row)
    sent_rows(3, outer_ref, p.k * (1 - last_row))
    sent_rows(3, inner_ref, 1 - p.k)
    copies_j[0].wait()
    for s in (1, 2, 0, 3):
        pltpu.make_async_copy(raw.at[s, :, middle], raw.at[s, :, middle], raw_sem.at[s, 0]).wait()
        pltpu.make_async_copy(raw.at[s, :, low], raw.at[s, :, low], raw_sem.at[s, 1]).wait()
        pltpu.make_async_copy(raw.at[s, :, high], raw.at[s, :, high], raw_sem.at[s, 2]).wait()
        turned = product(split(jr[s]), split(raw[s]))
        turned_high, turned_low = split(turned)
        half_high[s * BLK : (s + 1) * BLK] = turned_high
        half_low[s * BLK : (s + 1) * BLK] = turned_low
    copies_j[1].wait()
    stores = []
    for slots, panel in SLOTS:
        columns = pl.ds(panel * PAIR, PAIR)
        rotation = jc[slots[0]] if len(slots) == 1 else jnp.concatenate([jc[slots[0]], jc[slots[1]]], axis=1)
        turned = product((half_high[:, columns], half_low[:, columns]), split(rotation))
        for n, slot in enumerate(slots):
            result[slot] = turned[:, n * BLK : (n + 1) * BLK]
            store = pltpu.make_async_copy(result.at[slot], o_ref.at[:, pl.ds(slot * BLK, BLK)], out_sem.at[slot])
            store.start()
            stores.append(store)
    for store in stores:
        store.wait()


def apply(matrix, parts):
    any_spec = pl.BlockSpec(memory_space=pl.ANY)
    return pl.pallas_call(
        apply_kernel,
        out_shape=jax.ShapeDtypeStruct((ROWS, COLS), F32),
        in_specs=[any_spec] * 7,
        out_specs=any_spec,
        scratch_shapes=[
            pltpu.VMEM((4, PAIR, WIDE), F32),
            pltpu.VMEM((8, PAIR, BLK), F32),
            pltpu.VMEM((4, BLK, PAIR), F32),
            pltpu.VMEM((ROWS, WIDE), BF16),
            pltpu.VMEM((ROWS, WIDE), BF16),
            pltpu.VMEM((8, ROWS, BLK), F32),
            pltpu.SemaphoreType.DMA((4, 3)),
            pltpu.SemaphoreType.DMA((2,)),
            pltpu.SemaphoreType.DMA((8,)),
        ],
        compiler_params=pltpu.CompilerParams(vmem_limit_bytes=48 * 1024 * 1024),
        cost_estimate=pl.CostEstimate(flops=2 * 10**9, bytes_accessed=10**7, transcendentals=0),
        name="apply",
    )(matrix, *parts)


def local(matrix):
    return apply(matrix, travel(matrix))


def solution(mesh):
    spec = P("row", "col")
    return jax.shard_map(local, mesh=mesh, in_specs=(spec,), out_specs=spec, check_vma=False)
```

```python
import math

import jax
import jax.numpy as jnp
from jax import lax
from jax.experimental import pallas as pl
from jax.experimental.pallas import tpu as pltpu
from jax.sharding import PartitionSpec as P

MESH = pl.DeviceIdType.MESH
F32 = jnp.float32
BF16 = jnp.bfloat16
BLK = 128
PAIR = 256
INNER = 4
ROWS = 512
COLS = 1024
WIDE = COLS + 2 * PAIR
GROUPS = 16
FOLD = 264


def split(value):
    high = value.astype(BF16)
    return high, (value - high.astype(F32)).astype(BF16)


def product(first, second):
    (first_high, first_low), (second_high, second_low) = first, second
    left = jnp.concatenate([first_high, first_high, first_low], axis=1)
    right = jnp.concatenate([second_high, second_low, second_high], axis=0)
    return jnp.dot(left, right, preferred_element_type=F32)


def pair_rotation(square):
    i = lax.broadcasted_iota(jnp.int32, (PAIR, PAIR), 0)
    j = lax.broadcasted_iota(jnp.int32, (PAIR, PAIR), 1)
    weights = (j - i).astype(F32) * (0.25 / math.sqrt(PAIR) / (PAIR - 1))
    identity = jnp.where(i == j, 1.0, 0.0).astype(F32)
    current = square
    rotation = None
    for inner_step in range(INNER):
        last = inner_step == INNER - 1
        bracket = current * weights
        bracket_s = split(bracket)
        power = product(bracket_s, bracket_s)
        power_s = split(power)
        if not last:
            half = current + product(split(current), bracket_s)
        if rotation is None:
            turned = identity + bracket
        else:
            turned = rotation + product(split(rotation), bracket_s)
        power2 = product(power_s, power_s)
        if not last:
            both = half - product(bracket_s, split(half))
        series = 0.375 * identity + 0.3125 * power + 0.0625 * power2
        polish = split(0.5 * power + product(split(power2), split(series)))
        rotation = turned + product(split(turned), polish)
        if not last:
            half = both + product(split(both), polish)
            current = half + product(polish, split(half))
    return rotation


def fold(square):
    i = lax.broadcasted_iota(jnp.int32, (BLK, BLK), 0)
    j = lax.broadcasted_iota(jnp.int32, (BLK, BLK), 1)
    first, second = square[:BLK, :BLK], square[BLK:, BLK:]
    diagonal = jnp.sum(jnp.where(i == j, second, 0.0), axis=0, keepdims=True)
    return jnp.concatenate(
        [square[:BLK, BLK:], jnp.where(i <= j, first, second), jnp.broadcast_to(diagonal, (8, BLK))], axis=0
    )


def unfold(folded):
    i = lax.broadcasted_iota(jnp.int32, (BLK, BLK), 0)
    j = lax.broadcasted_iota(jnp.int32, (BLK, BLK), 1)
    side = folded[:BLK]
    middle = folded[BLK : 2 * BLK]
    flipped = middle.T
    first = jnp.where(i <= j, middle, flipped)
    second = jnp.where(i > j, middle, jnp.where(i < j, flipped, folded[2 * BLK : 2 * BLK + 1]))
    return jnp.concatenate(
        [jnp.concatenate([first, side], axis=1), jnp.concatenate([side.T, second], axis=1)], axis=0
    )


def choose(cond, yes, no):
    return cond * yes + (1 - cond) * no


def same(a, b):
    return int(a == b) if isinstance(a - b, int) else jnp.where(a == b, 1, 0)


def slot_of(group, member, half):
    step, slot = 0, 0
    for m, h, slot_in, step_in in (
        (0, 0, 2, 0), (1, 0, 4, 0), (2, 0, 6, 0), (3, 0, 0, 1),
        (0, 1, 7, -1), (1, 1, 1, 0), (2, 1, 3, 0), (3, 1, 5, 0),
    ):
        if h == half:
            slot = slot + same(member, m) * slot_in
            step = step + same(member, m) * step_in
    first, last = same(group, 0), same(group, GROUPS - 1)
    if half == 0:
        slot = slot - first * same(member, 0) * 2 + last * same(member, 3) * 7
        step = step - last * same(member, 3)
    else:
        slot = slot - first * same(member, 0) * 5
        step = step + first * same(member, 0)
    return step, slot


def maker_of(group, slot):
    step, member = {0: (-1, 3), 1: (0, 1), 2: (0, 0), 3: (0, 2), 4: (0, 1), 5: (0, 3), 6: (0, 2), 7: (1, 0)}[slot]
    if slot == 0:
        return choose(same(group, 0), 0, step), choose(same(group, 0), 0, member)
    if slot == 7:
        return choose(same(group, GROUPS - 1), 0, step), choose(same(group, GROUPS - 1), 3, member)
    return step, member


class Place:
    def __init__(self, row, col):
        self.row, self.c = row, col
        self.k, self.R = row % 2, row // 2
        self.x, self.zh = self.R % 4, self.R // 4
        self.y, self.zl = self.c % 4, self.c // 4
        self.on_diagonal = same(self.R, self.c)
        self.in_relay = same(self.zh, self.zl)
        self.turn = (self.zh - self.zl + 4) % 4

    def at(self, k=None, x=None, zh=None, y=None, zl=None):
        k = self.k if k is None else k
        x = self.x if x is None else x
        zh = self.zh if zh is None else zh
        y = self.y if y is None else y
        zl = self.zl if zl is None else zl
        return (2 * (4 * zh + x) + k, 4 * zl + y)


def scatter_out(p):
    found = []
    for j in range(2):
        q = 2 * p.k + j
        own = (1 - p.k) * same(p.x, q)
        found.append((j, "col", p.on_diagonal * own, p.on_diagonal * (1 - own), p.at(k=0, x=q)))
        own = p.k * same(p.y, q)
        found.append((j, "row", p.on_diagonal * own, p.on_diagonal * (1 - own), p.at(k=1, y=q)))
    return found


def cross_out(p):
    col = 1 - p.k
    up, down = p.at(zh=(p.zh + 1) % 4), p.at(zh=(p.zh + 3) % 4)
    found = [
        (col * same(p.turn, 0), up, 0),
        (col * same(p.turn, 0), down, 0),
        (col * same(p.turn, 1), up, 1),
        (col * same(p.turn, 3), down, 2),
    ]
    for t in range(1, 4):
        found.append((p.k * p.in_relay, p.at(zl=(p.zl + t) % 4), 0))
    return found


def spread_out(p):
    found = []
    for half in range(2):
        step, slot = slot_of(p.c, p.x, half)
        core, stays = slot % 2, same(step, 0)
        found.append(("col", half, 0, (1 - p.k) * (1 - stays), (2 * p.R + core, p.c + step), slot))
        for t in (2, 1, 3, 0):
            own = 1 - core if t == 0 else 0
            device = p.at(k=core, x=(p.x + t) % 4)
            found.append(("col", half, (1 - p.k) * stays * own, (1 - p.k) * stays * (1 - own), device, slot))
        step, slot = slot_of(p.R, p.y, half)
        core, stays = slot // 4, same(step, 0)
        found.append(("row", half, 0, p.k * (1 - stays), (2 * (p.R + step) + core, p.c), slot % 4))
        for t in (2, 1, 3, 0):
            own = core if t == 0 else 0
            device = p.at(k=core, y=(p.y + t) % 4)
            found.append(("row", half, p.k * stays * own, p.k * stays * (1 - own), device, slot % 4))
    return found


def hub_out(p):
    first, last = same(p.c, 0), same(p.c, GROUPS - 1)
    cond = choose(p.k, same(p.x, 0) * (1 - last), same(p.x, 3) * (1 - first))
    found = [("col", cond, 7 * p.k, [p.at(x=(p.x + t) % 4) for t in (2, 1, 3)])]
    first, last = same(p.R, 0), same(p.R, GROUPS - 1)
    cond = choose(p.k, same(p.y, 0) * (1 - last), same(p.y, 3) * (1 - first))
    found.append(("row", cond, 3 * p.k, [p.at(y=(p.y + t) % 4) for t in (2, 1, 3)]))
    return found


def outer_out(p):
    forward = p.k
    here = choose(forward, 1 - same(p.R, GROUPS - 1), 1 - same(p.R, 0))
    own_x = choose(forward, 3, 0)
    edge = same(p.x, own_x)
    next_row = (2 * (p.R + 2 * forward - 1) + 1 - p.k + 32) % 32
    found = []
    for q in range(4):
        relayed = here * edge * (1 - same(own_x, q))
        row = choose(relayed, p.at(x=q)[0], next_row)
        found.append((q, relayed, here * (1 - relayed), (row, p.c)))
    return found


def relay_role(p):
    forward = p.k
    own_x = choose(forward, 3, 0)
    inside = choose(forward, 1 - same(p.zh, 3), 1 - same(p.zh, 0))
    cond = inside * (1 - same(p.x, own_x))
    to_zh = (p.zh + choose(forward, 1, 3)) % 4
    return cond, p.at(k=1 - p.k, x=3 - own_x, zh=to_zh), p.at(x=own_x)


def edges_out(p):
    found = [(cond, device) for _, _, _, cond, device in scatter_out(p)]
    found += [(cond, device) for cond, device, _ in cross_out(p)]
    found += [(cond, device) for _, _, _, cond, device, _ in spread_out(p)]
    for _, cond, _, devices in hub_out(p):
        found += [(cond, device) for device in devices]
    for _, relayed, direct, device in outer_out(p):
        found.append((relayed + direct, device))
    cond, device, _ = relay_role(p)
    found.append((cond, device))
    found.append((1, p.at(k=1 - p.k)))
    found.append((1 - same(p.c, 0), (p.row, p.c - 1)))
    found.append((1 - same(p.c, GROUPS - 1), (p.row, p.c + 1)))
    return found


def edges_in(p):
    col = 1 - p.k
    source = p.at(k=p.x // 2, x=p.y)
    found = [(col * p.in_relay * (1 - same(p.x, p.y) * (1 - p.x // 2)), source)]
    source = p.at(k=p.y // 2, y=p.x)
    found.append((p.k * p.in_relay * (1 - same(p.x, p.y) * (p.y // 2)), source))
    up, down = p.at(zh=(p.zh + 1) % 4), p.at(zh=(p.zh + 3) % 4)
    found.append((col * (same(p.turn, 1) + same(p.turn, 2)), down))
    found.append((col * (same(p.turn, 3) + same(p.turn, 2)), up))
    found.append((p.k * (1 - p.in_relay), p.at(zl=p.zh)))
    for n in range(4):
        step, member = maker_of(p.c, 2 * n)
        step1, member1 = maker_of(p.c, 2 * n + 1)
        step, member = choose(p.k, step1, step), choose(p.k, member1, member)
        stays, own = same(step, 0), same(member, p.x)
        core = choose(stays, 0, choose(own, 0, p.k))
        found.append((1 - stays * own * (1 - p.k), (2 * (4 * p.zh + member) + core, p.c + own * step)))
        step, member = maker_of(p.R, n)
        step1, member1 = maker_of(p.R, 4 + n)
        step, member = choose(p.k, step1, step), choose(p.k, member1, member)
        stays, own = same(step, 0), same(member, p.y)
        core = choose(stays, 1, choose(own, 1, p.k))
        found.append((1 - stays * own * p.k, (2 * (p.R + own * step) + core, 4 * p.zl + member)))
    forward = 1 - p.k
    here = choose(forward, 1 - same(p.R, 0), 1 - same(p.R, GROUPS - 1))
    edge = same(p.x, choose(forward, 0, 3))
    source_row = (2 * (p.R + 1 - 2 * forward) + 1 - p.k + 32) % 32
    source_zh = source_row // 8
    for q in range(4):
        row = choose(edge, 8 * source_zh + 2 * q + 1 - p.k, source_row)
        found.append((here, (row, p.c)))
    relay, _, start = relay_role(p)
    found.append((relay, start))
    found.append((1, p.at(k=1 - p.k)))
    found.append((1 - same(p.c, 0), (p.row, p.c - 1)))
    found.append((1 - same(p.c, GROUPS - 1), (p.row, p.c + 1)))
    return found


def here():
    return Place(lax.axis_index("row"), lax.axis_index("col"))


def when(cond, action):
    if isinstance(cond, int):
        if cond:
            action()
    else:
        pl.when(cond == 1)(action)


class Sends:
    def __init__(self, sems):
        self.sems, self.pending = sems, []

    def start(self, cond, source, target, recv_sem, device):
        index = len(self.pending)

        def make():
            return pltpu.make_async_remote_copy(
                src_ref=source,
                dst_ref=target,
                send_sem=self.sems.at[index],
                recv_sem=recv_sem,
                device_id=device,
                device_id_type=MESH,
            )

        self.pending.append((cond, make))
        when(cond, lambda: make().start())

    def finish(self):
        for cond, make in self.pending:
            when(cond, lambda make=make: make().wait_send())


def arrived(ref, sem, cond=1):
    when(cond, lambda: pltpu.make_async_copy(ref, ref, sem).wait())


def travel_kernel(
    m_ref, left_ref, right_ref, outer_ref, inner_ref, jc_ref, jr_ref,
    square, folded, solver_in, out_c, out_r, relay,
    load_sem, send_sem, solver_sem, jc_sem, jr_sem, side_sem, outer_sem, outer_side_sem, inner_sem, relay_sem,
):
    p = here()
    loads = []
    for j in range(2):
        column = pl.multiple_of(p.k * ROWS + j * PAIR, PAIR)
        loads.append(
            pltpu.make_async_copy(
                m_ref.at[pl.ds(j * PAIR, PAIR), pl.ds(column, PAIR)], square.at[j], load_sem.at[j]
            )
        )
        when(p.on_diagonal, loads[j].start)

    barrier = pltpu.get_barrier_semaphore()
    for cond, device in edges_in(p):
        when(
            cond,
            lambda device=device: pl.semaphore_signal(barrier, inc=1, device_id=device, device_id_type=MESH),
        )

    def fold_both():
        for j in range(2):
            loads[j].wait()
            folded[j] = fold(square[j])

    when(p.on_diagonal, fold_both)
    pl.semaphore_wait(barrier, sum(cond for cond, _ in edges_out(p)))

    sends = Sends(send_sem)
    mate = p.at(k=1 - p.k)
    before, after = (p.row, p.c - 1), (p.row, p.c + 1)
    has_before, has_after = 1 - same(p.c, 0), 1 - same(p.c, GROUPS - 1)
    low = pl.multiple_of(p.k * PAIR, PAIR)
    other = pl.multiple_of((1 - p.k) * PAIR, PAIR)

    for j, _, own, cond, device in scatter_out(p):
        sends.start(cond, folded.at[j], solver_in, solver_sem.at[0], device)
        when(own, pltpu.make_async_copy(folded.at[j], solver_in, solver_sem.at[0]).start)

    sends.start(has_before, m_ref.at[:, pl.ds(0, PAIR)], right_ref, side_sem.at[1], before)
    sends.start(has_after, m_ref.at[:, pl.ds(COLS - PAIR, PAIR)], left_ref, side_sem.at[0], after)
    sends.start(1, m_ref.at[pl.ds(other, PAIR)], inner_ref.at[:, pl.ds(PAIR, COLS)], inner_sem.at[0], mate)
    for q, relayed, direct, device in outer_out(p):
        part = m_ref.at[pl.ds(low, PAIR), pl.ds(q * PAIR, PAIR)]
        sends.start(relayed, part, relay, relay_sem.at[0], device)
        sends.start(direct, part, outer_ref.at[:, pl.ds(PAIR + q * PAIR, PAIR)], outer_sem.at[q], device)

    whole = choose(1 - p.k, 1 - same(p.turn, 2), 1)
    halves = 1 - whole
    parts = (pl.ds(0, BLK), pl.ds(BLK, FOLD - BLK))
    arrived(solver_in, solver_sem.at[0], whole)
    for n in range(2):
        arrived(solver_in.at[parts[n]], solver_sem.at[1 + n], halves)
    for cond, device, part in cross_out(p):
        ref = solver_in if part == 0 else solver_in.at[parts[part - 1]]
        sends.start(cond, ref, ref, solver_sem.at[part], device)

    relaying, relay_to, _ = relay_role(p)
    arrived(relay, relay_sem.at[0], relaying)
    sends.start(
        relaying, relay, outer_ref.at[:, pl.ds(pl.multiple_of(PAIR + p.x * PAIR, PAIR), PAIR)], outer_sem.at[p.x], relay_to
    )

    rotation = pair_rotation(unfold(solver_in[...]))

    def keep_columns():
        for half in range(2):
            out_c[half] = rotation[:, half * BLK : (half + 1) * BLK]

    def keep_rows():
        flipped = rotation.T
        for half in range(2):
            out_r[half] = flipped[half * BLK : (half + 1) * BLK]

    when(1 - p.k, keep_columns)
    when(p.k, keep_rows)
    for kind, half, own, cond, device, slot in spread_out(p):
        source, target, sem = (out_c, jc_ref, jc_sem) if kind == "col" else (out_r, jr_ref, jr_sem)
        sends.start(cond, source.at[half], target.at[slot], sem.at[slot], device)
        if not isinstance(own, int):
            when(own, pltpu.make_async_copy(source.at[half], target.at[slot], sem.at[slot]).start)

    (_, hub, _, _), (_, hub_r, _, _) = hub_out(p)
    for kind, cond, slot, devices in hub_out(p):
        target, sem = (jc_ref, jc_sem) if kind == "col" else (jr_ref, jr_sem)
        arrived(target.at[slot], sem.at[slot], cond)
        for device in devices:
            sends.start(cond, target.at[slot], target.at[slot], sem.at[slot], device)

    arrived(left_ref, side_sem.at[0], has_before)
    sends.start(has_before, left_ref.at[pl.ds(other, PAIR)], inner_ref.at[:, pl.ds(0, PAIR)], inner_sem.at[1], mate)
    arrived(right_ref, side_sem.at[1], has_after)
    sends.start(
        has_after, right_ref.at[pl.ds(other, PAIR)], inner_ref.at[:, pl.ds(PAIR + COLS, PAIR)], inner_sem.at[2], mate
    )
    has_outer = choose(p.k, 1 - same(p.R, GROUPS - 1), 1 - same(p.R, 0))
    for q in range(4):
        arrived(outer_ref.at[:, pl.ds(PAIR + q * PAIR, PAIR)], outer_sem.at[q], has_outer)
        if q == 0:
            sends.start(
                has_outer * has_before, outer_ref.at[:, pl.ds(PAIR, PAIR)], outer_ref.at[:, pl.ds(PAIR + COLS, PAIR)],
                outer_side_sem.at[1], before,
            )
    sends.start(
        has_outer * has_after, outer_ref.at[:, pl.ds(COLS, PAIR)], outer_ref.at[:, pl.ds(0, PAIR)],
        outer_side_sem.at[0], after,
    )

    for n in range(4):
        slot = 2 * n + p.k
        arrived(jc_ref.at[slot], jc_sem.at[slot], 1 - hub * same(slot, 7 * p.k))
        sends.start(1, jc_ref.at[slot], jc_ref.at[slot], jc_sem.at[slot], mate)
    for n in range(4):
        arrived(jc_ref.at[2 * n + 1 - p.k], jc_sem.at[2 * n + 1 - p.k])
        arrived(jr_ref.at[n], jr_sem.at[n], 1 - hub_r * same(n, 3 * p.k))

    arrived(inner_ref.at[:, pl.ds(PAIR, COLS)], inner_sem.at[0])
    arrived(inner_ref.at[:, pl.ds(0, PAIR)], inner_sem.at[1], has_before)
    arrived(inner_ref.at[:, pl.ds(PAIR + COLS, PAIR)], inner_sem.at[2], has_after)
    arrived(outer_ref.at[:, pl.ds(0, PAIR)], outer_side_sem.at[0], has_outer * has_before)
    arrived(outer_ref.at[:, pl.ds(PAIR + COLS, PAIR)], outer_side_sem.at[1], has_outer * has_after)
    sends.finish()


def travel(matrix):
    any_spec = pl.BlockSpec(memory_space=pltpu.HBM)
    shapes = [(ROWS, PAIR), (ROWS, PAIR), (PAIR, WIDE), (PAIR, WIDE), (8, PAIR, BLK), (4, BLK, PAIR)]
    return pl.pallas_call(
        travel_kernel,
        out_shape=[jax.ShapeDtypeStruct(shape, F32) for shape in shapes],
        in_specs=[any_spec],
        out_specs=[any_spec] * len(shapes),
        scratch_shapes=[
            pltpu.VMEM((2, PAIR, PAIR), F32),
            pltpu.VMEM((2, FOLD, BLK), F32),
            pltpu.VMEM((FOLD, BLK), F32),
            pltpu.VMEM((2, PAIR, BLK), F32),
            pltpu.VMEM((2, BLK, PAIR), F32),
            pltpu.VMEM((PAIR, PAIR), F32),
            pltpu.SemaphoreType.DMA((2,)),
            pltpu.SemaphoreType.DMA((80,)),
            pltpu.SemaphoreType.DMA((3,)),
            pltpu.SemaphoreType.DMA((8,)),
            pltpu.SemaphoreType.DMA((4,)),
            pltpu.SemaphoreType.DMA((2,)),
            pltpu.SemaphoreType.DMA((4,)),
            pltpu.SemaphoreType.DMA((2,)),
            pltpu.SemaphoreType.DMA((3,)),
            pltpu.SemaphoreType.DMA((1,)),
        ],
        compiler_params=pltpu.CompilerParams(
            collective_id=1, has_side_effects=True, vmem_limit_bytes=32 * 1024 * 1024
        ),
        cost_estimate=pl.CostEstimate(flops=10**9, bytes_accessed=10**7, transcendentals=0),
        name="travel",
    )(matrix)


SLOTS = (((0,), 0), ((1, 4), 2), ((2,), 1), ((3, 6), 3), ((5,), 4), ((7,), 5))


def apply_kernel(
    m_ref, left_ref, right_ref, outer_ref, inner_ref, jc_ref, jr_ref, o_ref, raw, jc, jr, half_high, half_low, result,
    raw_sem, j_sem, out_sem,
):
    p = here()
    first_col, last_col = same(p.c, 0), same(p.c, GROUPS - 1)
    first_row, last_row = same(p.row, 0), same(p.row, 2 * GROUPS - 1)
    copies_j = [
        pltpu.make_async_copy(jr_ref, jr, j_sem.at[0]),
        pltpu.make_async_copy(jc_ref, jc, j_sem.at[1]),
    ]
    for copy in copies_j:
        copy.start()
    low, middle, high = pl.ds(0, PAIR), pl.ds(PAIR, COLS), pl.ds(PAIR + COLS, PAIR)

    def own_rows(s, pair, cond):
        rows = pl.ds(pair * PAIR, PAIR)
        when(cond, pltpu.make_async_copy(m_ref.at[rows], raw.at[s, :, middle], raw_sem.at[s, 0]).start)
        when(cond * (1 - first_col), pltpu.make_async_copy(left_ref.at[rows], raw.at[s, :, low], raw_sem.at[s, 1]).start)
        when(cond * (1 - last_col), pltpu.make_async_copy(right_ref.at[rows], raw.at[s, :, high], raw_sem.at[s, 2]).start)
        when(
            cond * first_col,
            pltpu.make_async_copy(m_ref.at[rows, pl.ds(0, PAIR)], raw.at[s, :, low], raw_sem.at[s, 1]).start,
        )
        when(
            cond * last_col,
            pltpu.make_async_copy(m_ref.at[rows, pl.ds(COLS - PAIR, PAIR)], raw.at[s, :, high], raw_sem.at[s, 2]).start,
        )

    def sent_rows(s, ref, cond):
        when(cond, pltpu.make_async_copy(ref.at[:, middle], raw.at[s, :, middle], raw_sem.at[s, 0]).start)
        when(cond * (1 - first_col), pltpu.make_async_copy(ref.at[:, low], raw.at[s, :, low], raw_sem.at[s, 1]).start)
        when(cond * (1 - last_col), pltpu.make_async_copy(ref.at[:, high], raw.at[s, :, high], raw_sem.at[s, 2]).start)
        when(
            cond * first_col,
            pltpu.make_async_copy(ref.at[:, pl.ds(PAIR, PAIR)], raw.at[s, :, low], raw_sem.at[s, 1]).start,
        )
        when(
            cond * last_col,
            pltpu.make_async_copy(ref.at[:, pl.ds(COLS, PAIR)], raw.at[s, :, high], raw_sem.at[s, 2]).start,
        )

    own_rows(1, 1, 1)
    own_rows(2, 0, 1)
    own_rows(0, 0, first_row)
    sent_rows(0, outer_ref, (1 - p.k) * (1 - first_row))
    sent_rows(0, inner_ref, p.k)
    own_rows(3, 1, last_row)
    sent_rows(3, outer_ref, p.k * (1 - last_row))
    sent_rows(3, inner_ref, 1 - p.k)
    copies_j[0].wait()
    for s in (1, 2, 0, 3):
        pltpu.make_async_copy(raw.at[s, :, middle], raw.at[s, :, middle], raw_sem.at[s, 0]).wait()
        pltpu.make_async_copy(raw.at[s, :, low], raw.at[s, :, low], raw_sem.at[s, 1]).wait()
        pltpu.make_async_copy(raw.at[s, :, high], raw.at[s, :, high], raw_sem.at[s, 2]).wait()
        turned = product(split(jr[s]), split(raw[s]))
        turned_high, turned_low = split(turned)
        half_high[s * BLK : (s + 1) * BLK] = turned_high
        half_low[s * BLK : (s + 1) * BLK] = turned_low
    copies_j[1].wait()
    stores = []
    for slots, panel in SLOTS:
        columns = pl.ds(panel * PAIR, PAIR)
        rotation = jc[slots[0]] if len(slots) == 1 else jnp.concatenate([jc[slots[0]], jc[slots[1]]], axis=1)
        turned = product((half_high[:, columns], half_low[:, columns]), split(rotation))
        for n, slot in enumerate(slots):
            result[slot] = turned[:, n * BLK : (n + 1) * BLK]
            store = pltpu.make_async_copy(result.at[slot], o_ref.at[:, pl.ds(slot * BLK, BLK)], out_sem.at[slot])
            store.start()
            stores.append(store)
    for store in stores:
        store.wait()


def apply(matrix, parts):
    any_spec = pl.BlockSpec(memory_space=pltpu.HBM)
    return pl.pallas_call(
        apply_kernel,
        out_shape=jax.ShapeDtypeStruct((ROWS, COLS), F32),
        in_specs=[any_spec] * 7,
        out_specs=any_spec,
        scratch_shapes=[
            pltpu.VMEM((4, PAIR, WIDE), F32),
            pltpu.VMEM((8, PAIR, BLK), F32),
            pltpu.VMEM((4, BLK, PAIR), F32),
            pltpu.VMEM((ROWS, WIDE), BF16),
            pltpu.VMEM((ROWS, WIDE), BF16),
            pltpu.VMEM((8, ROWS, BLK), F32),
            pltpu.SemaphoreType.DMA((4, 3)),
            pltpu.SemaphoreType.DMA((2,)),
            pltpu.SemaphoreType.DMA((8,)),
        ],
        compiler_params=pltpu.CompilerParams(vmem_limit_bytes=48 * 1024 * 1024),
        cost_estimate=pl.CostEstimate(flops=2 * 10**9, bytes_accessed=10**7, transcendentals=0),
        name="apply",
    )(matrix, *parts)


def local(matrix):
    return apply(matrix, travel(matrix))


def solution(mesh):
    spec = P("row", "col")
    return jax.shard_map(local, mesh=mesh, in_specs=(spec,), out_specs=spec, check_vma=False)
```

```python
import math

import jax
import jax.numpy as jnp
from jax import lax
from jax.experimental import pallas as pl
from jax.experimental.pallas import tpu as pltpu
from jax.sharding import PartitionSpec as P

MESH = pl.DeviceIdType.MESH
F32 = jnp.float32
BF16 = jnp.bfloat16
BLK = 128
PAIR = 256
INNER = 4
ROWS = 512
COLS = 1024
WIDE = COLS + 2 * PAIR
GROUPS = 16
FOLD = 264


def split(value):
    high = value.astype(BF16)
    return high, (value - high.astype(F32)).astype(BF16)


def product(first, second):
    (first_high, first_low), (second_high, second_low) = first, second
    left = jnp.concatenate([first_high, first_high, first_low], axis=1)
    right = jnp.concatenate([second_high, second_low, second_high], axis=0)
    return jnp.dot(left, right, preferred_element_type=F32)


def pair_rotation(square):
    i = lax.broadcasted_iota(jnp.int32, (PAIR, PAIR), 0)
    j = lax.broadcasted_iota(jnp.int32, (PAIR, PAIR), 1)
    weights = (j - i).astype(F32) * (0.25 / math.sqrt(PAIR) / (PAIR - 1))
    identity = jnp.where(i == j, 1.0, 0.0).astype(F32)
    current = square
    rotation = None
    for inner_step in range(INNER):
        last = inner_step == INNER - 1
        bracket = current * weights
        bracket_s = split(bracket)
        power = product(bracket_s, bracket_s)
        power_s = split(power)
        if not last:
            half = current + product(split(current), bracket_s)
        if rotation is None:
            turned = identity + bracket
        else:
            turned = rotation + product(split(rotation), bracket_s)
        power2 = product(power_s, power_s)
        if not last:
            both = half - product(bracket_s, split(half))
        series = 0.375 * identity + 0.3125 * power + 0.0625 * power2
        polish = split(0.5 * power + product(split(power2), split(series)))
        rotation = turned + product(split(turned), polish)
        if not last:
            half = both + product(split(both), polish)
            current = half + product(polish, split(half))
    return rotation


def fold(square):
    i = lax.broadcasted_iota(jnp.int32, (BLK, BLK), 0)
    j = lax.broadcasted_iota(jnp.int32, (BLK, BLK), 1)
    first, second = square[:BLK, :BLK], square[BLK:, BLK:]
    diagonal = jnp.sum(jnp.where(i == j, second, 0.0), axis=0, keepdims=True)
    return jnp.concatenate(
        [square[:BLK, BLK:], jnp.where(i <= j, first, second), jnp.broadcast_to(diagonal, (8, BLK))], axis=0
    )


def unfold(folded):
    i = lax.broadcasted_iota(jnp.int32, (BLK, BLK), 0)
    j = lax.broadcasted_iota(jnp.int32, (BLK, BLK), 1)
    side = folded[:BLK]
    middle = folded[BLK : 2 * BLK]
    flipped = middle.T
    first = jnp.where(i <= j, middle, flipped)
    second = jnp.where(i > j, middle, jnp.where(i < j, flipped, folded[2 * BLK : 2 * BLK + 1]))
    return jnp.concatenate(
        [jnp.concatenate([first, side], axis=1), jnp.concatenate([side.T, second], axis=1)], axis=0
    )


def choose(cond, yes, no):
    return cond * yes + (1 - cond) * no


def same(a, b):
    return int(a == b) if isinstance(a - b, int) else jnp.where(a == b, 1, 0)


def slot_of(group, member, half):
    step, slot = 0, 0
    for m, h, slot_in, step_in in (
        (0, 0, 2, 0), (1, 0, 4, 0), (2, 0, 6, 0), (3, 0, 0, 1),
        (0, 1, 7, -1), (1, 1, 1, 0), (2, 1, 3, 0), (3, 1, 5, 0),
    ):
        if h == half:
            slot = slot + same(member, m) * slot_in
            step = step + same(member, m) * step_in
    first, last = same(group, 0), same(group, GROUPS - 1)
    if half == 0:
        slot = slot - first * same(member, 0) * 2 + last * same(member, 3) * 7
        step = step - last * same(member, 3)
    else:
        slot = slot - first * same(member, 0) * 5
        step = step + first * same(member, 0)
    return step, slot


def maker_of(group, slot):
    step, member = {0: (-1, 3), 1: (0, 1), 2: (0, 0), 3: (0, 2), 4: (0, 1), 5: (0, 3), 6: (0, 2), 7: (1, 0)}[slot]
    if slot == 0:
        return choose(same(group, 0), 0, step), choose(same(group, 0), 0, member)
    if slot == 7:
        return choose(same(group, GROUPS - 1), 0, step), choose(same(group, GROUPS - 1), 3, member)
    return step, member


class Place:
    def __init__(self, row, col):
        self.row, self.c = row, col
        self.k, self.R = row % 2, row // 2
        self.x, self.zh = self.R % 4, self.R // 4
        self.y, self.zl = self.c % 4, self.c // 4
        self.on_diagonal = same(self.R, self.c)
        self.in_relay = same(self.zh, self.zl)

    def at(self, k=None, x=None, zh=None, y=None, zl=None):
        k = self.k if k is None else k
        x = self.x if x is None else x
        zh = self.zh if zh is None else zh
        y = self.y if y is None else y
        zl = self.zl if zl is None else zl
        return (2 * (4 * zh + x) + k, 4 * zl + y)


def scatter_out(p):
    found = []
    for j in range(2):
        q = 2 * p.k + j
        own = (1 - p.k) * same(p.x, q)
        found.append((j, "col", p.on_diagonal * own, p.on_diagonal * (1 - own), p.at(k=0, x=q)))
        own = p.k * same(p.y, q)
        found.append((j, "row", p.on_diagonal * own, p.on_diagonal * (1 - own), p.at(k=1, y=q)))
    return found


def cross_out(p):
    found = []
    for t in (2, 1, 3):
        row = choose(p.k, p.row, p.at(zh=(p.zh + t) % 4)[0])
        col = choose(p.k, p.at(zl=(p.zl + t) % 4)[1], p.c)
        found.append((p.in_relay, (row, col)))
    return found


def spread_out(p):
    found = []
    for half in range(2):
        step, slot = slot_of(p.c, p.x, half)
        core, stays = slot % 2, same(step, 0)
        found.append(("col", half, 0, (1 - p.k) * (1 - stays), (2 * p.R + core, p.c + step), slot))
        for t in (2, 1, 3, 0):
            own = 1 - core if t == 0 else 0
            device = p.at(k=core, x=(p.x + t) % 4)
            found.append(("col", half, (1 - p.k) * stays * own, (1 - p.k) * stays * (1 - own), device, slot))
        step, slot = slot_of(p.R, p.y, half)
        core, stays = slot // 4, same(step, 0)
        found.append(("row", half, 0, p.k * (1 - stays), (2 * (p.R + step) + core, p.c), slot % 4))
        for t in (2, 1, 3, 0):
            own = core if t == 0 else 0
            device = p.at(k=core, y=(p.y + t) % 4)
            found.append(("row", half, p.k * stays * own, p.k * stays * (1 - own), device, slot % 4))
    return found


def hub_out(p):
    first, last = same(p.c, 0), same(p.c, GROUPS - 1)
    cond = choose(p.k, same(p.x, 0) * (1 - last), same(p.x, 3) * (1 - first))
    found = [("col", cond, 7 * p.k, [p.at(x=(p.x + t) % 4) for t in (2, 1, 3)])]
    first, last = same(p.R, 0), same(p.R, GROUPS - 1)
    cond = choose(p.k, same(p.y, 0) * (1 - last), same(p.y, 3) * (1 - first))
    found.append(("row", cond, 3 * p.k, [p.at(y=(p.y + t) % 4) for t in (2, 1, 3)]))
    return found


def outer_out(p):
    forward = p.k
    here = choose(forward, 1 - same(p.R, GROUPS - 1), 1 - same(p.R, 0))
    own_x = choose(forward, 3, 0)
    edge = same(p.x, own_x)
    next_row = (2 * (p.R + 2 * forward - 1) + 1 - p.k + 32) % 32
    found = []
    for q in range(4):
        relayed = here * edge * (1 - same(own_x, q))
        row = choose(relayed, p.at(x=q)[0], next_row)
        found.append((q, relayed, here * (1 - relayed), (row, p.c)))
    return found


def relay_role(p):
    forward = p.k
    own_x = choose(forward, 3, 0)
    inside = choose(forward, 1 - same(p.zh, 3), 1 - same(p.zh, 0))
    cond = inside * (1 - same(p.x, own_x))
    to_zh = (p.zh + choose(forward, 1, 3)) % 4
    return cond, p.at(k=1 - p.k, x=3 - own_x, zh=to_zh), p.at(x=own_x)


def side_out(p):
    found = []
    for side in range(2):
        exists = 1 - same(p.c, 0 if side else GROUPS - 1)
        own_y = 0 if side else 3
        crosses = same(p.y, own_y)
        for q in range(4):
            relayed = 0 if q == own_y else exists * crosses
            col = p.c + 1 - 2 * side
            if q != own_y:
                col = choose(relayed, p.at(y=q)[1], col)
            found.append((side, q, relayed, exists * (1 - relayed), (p.row, col)))
    return found


def side_relay(p):
    found = []
    for side in range(2):
        own_y = 0 if side else 3
        cond = (1 - same(p.zl, 0 if side else 3)) * (1 - same(p.y, own_y))
        found.append((side, cond, p.at(y=3 - own_y, zl=(p.zl + (3 if side else 1)) % 4), p.at(y=own_y)))
    return found


def edges_out(p):
    found = cross_out(p)
    found += [(cond, device) for _, _, _, cond, device, _ in spread_out(p)]
    for _, cond, _, devices in hub_out(p):
        found += [(cond, device) for device in devices]
    for _, relayed, direct, device in outer_out(p):
        found.append((relayed + direct, device))
    cond, device, _ = relay_role(p)
    found.append((cond, device))
    found.append((1, p.at(k=1 - p.k)))
    found += [(relayed + direct, device) for _, _, relayed, direct, device in side_out(p)]
    found += [(cond, device) for _, cond, device, _ in side_relay(p)]
    return found


def first_edges_out(p):
    return [(cond, device) for _, _, _, cond, device in scatter_out(p)]


def first_edges_in(p):
    member, source_x, source_y = choose(p.k, p.y, p.x), choose(p.k, p.x, p.y), choose(p.k, p.x, p.y)
    own = p.on_diagonal * same(p.k, member // 2)
    return [(p.in_relay * (1 - own), p.at(k=member // 2, x=source_x, y=source_y))]


def edges_in(p):
    source = choose(p.k, p.row, p.at(zh=p.zl)[0]), choose(p.k, p.at(zl=p.zh)[1], p.c)
    found = [(1 - p.in_relay, source)]
    for n in range(4):
        step, member = maker_of(p.c, 2 * n)
        step1, member1 = maker_of(p.c, 2 * n + 1)
        step, member = choose(p.k, step1, step), choose(p.k, member1, member)
        stays, own = same(step, 0), same(member, p.x)
        core = choose(stays, 0, choose(own, 0, p.k))
        found.append((1 - stays * own * (1 - p.k), (2 * (4 * p.zh + member) + core, p.c + own * step)))
        step, member = maker_of(p.R, n)
        step1, member1 = maker_of(p.R, 4 + n)
        step, member = choose(p.k, step1, step), choose(p.k, member1, member)
        stays, own = same(step, 0), same(member, p.y)
        core = choose(stays, 1, choose(own, 1, p.k))
        found.append((1 - stays * own * p.k, (2 * (p.R + own * step) + core, 4 * p.zl + member)))
    forward = 1 - p.k
    here = choose(forward, 1 - same(p.R, 0), 1 - same(p.R, GROUPS - 1))
    edge = same(p.x, choose(forward, 0, 3))
    source_row = (2 * (p.R + 1 - 2 * forward) + 1 - p.k + 32) % 32
    source_zh = source_row // 8
    for q in range(4):
        row = choose(edge, 8 * source_zh + 2 * q + 1 - p.k, source_row)
        found.append((here, (row, p.c)))
    relay, _, start = relay_role(p)
    found.append((relay, start))
    found.append((1, p.at(k=1 - p.k)))
    for side, cond, _, source in side_relay(p):
        found.append((cond, source))
        own_y = 0 if side else 3
        exists, crosses = 1 - same(p.c, GROUPS - 1 if side else 0), same(p.y, 3 - own_y)
        for q in range(4):
            col = choose(crosses, p.at(y=q, zl=(p.zl + (1 if side else 3)) % 4)[1], p.c - 1 + 2 * side)
            found.append((exists, (p.row, col)))
    return found


def here():
    return Place(lax.axis_index("row"), lax.axis_index("col"))


def when(cond, action):
    if isinstance(cond, int):
        if cond:
            action()
    else:
        pl.when(cond == 1)(action)


class Sends:
    def __init__(self, sems):
        self.sems, self.pending = sems, []

    def start(self, cond, source, target, recv_sem, device):
        index = len(self.pending)

        def make():
            return pltpu.make_async_remote_copy(
                src_ref=source,
                dst_ref=target,
                send_sem=self.sems.at[index],
                recv_sem=recv_sem,
                device_id=device,
                device_id_type=MESH,
            )

        self.pending.append((cond, make))
        when(cond, lambda: make().start())

    def finish(self):
        for cond, make in self.pending:
            when(cond, lambda make=make: make().wait_send())


def arrived(ref, sem, cond=1):
    when(cond, lambda: pltpu.make_async_copy(ref, ref, sem).wait())


def greet(edges_in, edges_out):
    barrier = pltpu.get_barrier_semaphore()
    for cond, device in edges_in:
        when(
            cond,
            lambda device=device: pl.semaphore_signal(barrier, inc=1, device_id=device, device_id_type=MESH),
        )
    count = sum(cond for cond, _ in edges_out)
    pl.when(count > 0)(lambda: pl.semaphore_wait(barrier, count))


def first_kernel(m_ref, out_ref, square, folded, received, load_sem, send_sem, receive_sem):
    p = here()
    loads = []
    for j in range(2):
        column = pl.multiple_of(p.k * ROWS + j * PAIR, PAIR)
        loads.append(
            pltpu.make_async_copy(
                m_ref.at[pl.ds(j * PAIR, PAIR), pl.ds(column, PAIR)], square.at[j], load_sem.at[j]
            )
        )
        when(p.on_diagonal, loads[j].start)

    def fold_both():
        for j in range(2):
            loads[j].wait()
            folded[j] = fold(square[j])

    when(p.on_diagonal, fold_both)
    greet(first_edges_in(p), first_edges_out(p))
    sends = Sends(send_sem)
    for j, _, own, cond, device in scatter_out(p):
        sends.start(cond, folded.at[j], received, receive_sem.at[0], device)
        when(own, pltpu.make_async_copy(folded.at[j], received, receive_sem.at[0]).start)

    def keep():
        pltpu.make_async_copy(received, received, receive_sem.at[0]).wait()
        out_ref[...] = received[...]

    when(p.in_relay, keep)
    when(1 - p.in_relay, lambda: out_ref.__setitem__(..., jnp.zeros((FOLD, BLK), F32)))
    sends.finish()


def travel_kernel(
    m_ref, first_ref, left_ref, right_ref, outer_ref, inner_ref, jc_ref, jr_ref,
    solver_in, out_c, out_r, relay, side_pass,
    send_sem, solver_sem, jc_sem, jr_sem, side_sem, outer_sem, outer_side_sem, inner_sem, relay_sem, side_pass_sem,
):
    p = here()
    greet(edges_in(p), edges_out(p))
    sends = Sends(send_sem)
    mate = p.at(k=1 - p.k)
    before, after = (p.row, p.c - 1), (p.row, p.c + 1)
    has_before, has_after = 1 - same(p.c, 0), 1 - same(p.c, GROUPS - 1)
    low = pl.multiple_of(p.k * PAIR, PAIR)
    other = pl.multiple_of((1 - p.k) * PAIR, PAIR)

    for cond, device in cross_out(p):
        sends.start(cond, first_ref, solver_in, solver_sem.at[0], device)

    sides = (left_ref, right_ref)
    for side, q, relayed, direct, device in side_out(p):
        part = m_ref.at[pl.ds(q * BLK, BLK), pl.ds(0 if side else COLS - PAIR, PAIR)]
        if not isinstance(relayed, int):
            sends.start(relayed, part, side_pass.at[side], side_pass_sem.at[side], device)
        sends.start(direct, part, sides[side].at[pl.ds(q * BLK, BLK)], side_sem.at[side, q], device)
    sends.start(1, m_ref.at[pl.ds(other, PAIR)], inner_ref.at[:, pl.ds(PAIR, COLS)], inner_sem.at[0], mate)
    for q, relayed, direct, device in outer_out(p):
        part = m_ref.at[pl.ds(low, PAIR), pl.ds(q * PAIR, PAIR)]
        sends.start(relayed, part, relay, relay_sem.at[0], device)
        sends.start(direct, part, outer_ref.at[:, pl.ds(PAIR + q * PAIR, PAIR)], outer_sem.at[q], device)

    for side, cond, device, _ in side_relay(p):
        arrived(side_pass.at[side], side_pass_sem.at[side], cond)
        part = pl.ds(pl.multiple_of(p.y * BLK, BLK), BLK)
        sends.start(cond, side_pass.at[side], sides[side].at[part], side_sem.at[side, p.y], device)
    relaying, relay_to, _ = relay_role(p)
    arrived(relay, relay_sem.at[0], relaying)
    sends.start(
        relaying, relay, outer_ref.at[:, pl.ds(pl.multiple_of(PAIR + p.x * PAIR, PAIR), PAIR)], outer_sem.at[p.x], relay_to
    )

    arrived(solver_in, solver_sem.at[0], 1 - p.in_relay)
    rotation = pair_rotation(unfold(jnp.where(p.in_relay == 1, first_ref[...], solver_in[...])))

    def keep_columns():
        for half in range(2):
            out_c[half] = rotation[:, half * BLK : (half + 1) * BLK]

    def keep_rows():
        flipped = rotation.T
        for half in range(2):
            out_r[half] = flipped[half * BLK : (half + 1) * BLK]

    when(1 - p.k, keep_columns)
    when(p.k, keep_rows)
    for kind, half, own, cond, device, slot in spread_out(p):
        source, target, sem = (out_c, jc_ref, jc_sem) if kind == "col" else (out_r, jr_ref, jr_sem)
        sends.start(cond, source.at[half], target.at[slot], sem.at[slot], device)
        if not isinstance(own, int):
            when(own, pltpu.make_async_copy(source.at[half], target.at[slot], sem.at[slot]).start)

    (_, hub, _, _), (_, hub_r, _, _) = hub_out(p)
    for kind, cond, slot, devices in hub_out(p):
        target, sem = (jc_ref, jc_sem) if kind == "col" else (jr_ref, jr_sem)
        arrived(target.at[slot], sem.at[slot], cond)
        for device in devices:
            sends.start(cond, target.at[slot], target.at[slot], sem.at[slot], device)

    has_outer = choose(p.k, 1 - same(p.R, GROUPS - 1), 1 - same(p.R, 0))
    sends_on = choose(p.k, 1 - same(p.x, 3), 1 - same(p.x, 0))
    (_, _, _, next_device), *_ = outer_out(p)
    ends = (pl.ds(0, PAIR), pl.ds(PAIR + COLS, PAIR))
    for side, exists, edge_y in ((0, has_before, 0), (1, has_after, 3)):
        for q in range(4):
            arrived(sides[side].at[pl.ds(q * BLK, BLK)], side_sem.at[side, q], exists)
        sends.start(
            exists, sides[side].at[pl.ds(other, PAIR)], inner_ref.at[:, ends[side]], inner_sem.at[1 + side], mate
        )
        sends.start(
            sends_on * exists * same(p.y, edge_y), sides[side].at[pl.ds(low, PAIR)], outer_ref.at[:, ends[side]],
            outer_side_sem.at[side], next_device,
        )
    for q in range(4):
        arrived(outer_ref.at[:, pl.ds(PAIR + q * PAIR, PAIR)], outer_sem.at[q], has_outer)
        if q == 0:
            sends.start(
                has_outer * has_before * (1 - sends_on * same(p.y, 0)), outer_ref.at[:, pl.ds(PAIR, PAIR)],
                outer_ref.at[:, ends[1]], outer_side_sem.at[1], before,
            )
    sends.start(
        has_outer * has_after * (1 - sends_on * same(p.y, 3)), outer_ref.at[:, pl.ds(COLS, PAIR)],
        outer_ref.at[:, ends[0]], outer_side_sem.at[0], after,
    )

    for n in (1, 2, 3, 0):
        slot = choose(p.k, (1, 3, 5, 7)[n - 1], 2 * n)
        arrived(jc_ref.at[slot], jc_sem.at[slot], 1 - hub * same(slot, 7 * p.k))
        sends.start(1, jc_ref.at[slot], jc_ref.at[slot], jc_sem.at[slot], mate)
    for n in range(4):
        arrived(jc_ref.at[2 * n + 1 - p.k], jc_sem.at[2 * n + 1 - p.k])
        arrived(jr_ref.at[n], jr_sem.at[n], 1 - hub_r * same(n, 3 * p.k))

    arrived(inner_ref.at[:, pl.ds(PAIR, COLS)], inner_sem.at[0])
    arrived(inner_ref.at[:, pl.ds(0, PAIR)], inner_sem.at[1], has_before)
    arrived(inner_ref.at[:, pl.ds(PAIR + COLS, PAIR)], inner_sem.at[2], has_after)
    arrived(outer_ref.at[:, pl.ds(0, PAIR)], outer_side_sem.at[0], has_outer * has_before)
    arrived(outer_ref.at[:, pl.ds(PAIR + COLS, PAIR)], outer_side_sem.at[1], has_outer * has_after)
    sends.finish()


MIB = 1024 * 1024


def first(matrix):
    return pl.pallas_call(
        first_kernel,
        out_shape=jax.ShapeDtypeStruct((FOLD, BLK), F32),
        in_specs=[pl.BlockSpec(memory_space=pltpu.HBM)],
        out_specs=pl.BlockSpec(memory_space=pltpu.VMEM),
        scratch_shapes=[
            pltpu.VMEM((2, PAIR, PAIR), F32),
            pltpu.VMEM((2, FOLD, BLK), F32),
            pltpu.VMEM((FOLD, BLK), F32),
            pltpu.SemaphoreType.DMA((2,)),
            pltpu.SemaphoreType.DMA((4,)),
            pltpu.SemaphoreType.DMA((1,)),
        ],
        compiler_params=pltpu.CompilerParams(collective_id=0, has_side_effects=True, vmem_limit_bytes=62 * MIB),
        cost_estimate=pl.CostEstimate(flops=10**6, bytes_accessed=10**6, transcendentals=0),
        name="first",
    )(matrix)


def travel(matrix, folded):
    any_spec = pl.BlockSpec(memory_space=pl.ANY)
    shapes = [(ROWS, PAIR), (ROWS, PAIR), (PAIR, WIDE), (PAIR, WIDE), (8, PAIR, BLK), (4, BLK, PAIR)]
    return pl.pallas_call(
        travel_kernel,
        out_shape=[jax.ShapeDtypeStruct(shape, F32) for shape in shapes],
        in_specs=[pl.BlockSpec(memory_space=pltpu.HBM), pl.BlockSpec(memory_space=pltpu.VMEM)],
        out_specs=[any_spec] * len(shapes),
        scratch_shapes=[
            pltpu.VMEM((FOLD, BLK), F32),
            pltpu.VMEM((2, PAIR, BLK), F32),
            pltpu.VMEM((2, BLK, PAIR), F32),
            pltpu.VMEM((PAIR, PAIR), F32),
            pltpu.VMEM((2, BLK, PAIR), F32),
            pltpu.SemaphoreType.DMA((96,)),
            pltpu.SemaphoreType.DMA((1,)),
            pltpu.SemaphoreType.DMA((8,)),
            pltpu.SemaphoreType.DMA((4,)),
            pltpu.SemaphoreType.DMA((2, 4)),
            pltpu.SemaphoreType.DMA((4,)),
            pltpu.SemaphoreType.DMA((2,)),
            pltpu.SemaphoreType.DMA((3,)),
            pltpu.SemaphoreType.DMA((1,)),
            pltpu.SemaphoreType.DMA((2,)),
        ],
        compiler_params=pltpu.CompilerParams(collective_id=1, has_side_effects=True, vmem_limit_bytes=32 * MIB),
        cost_estimate=pl.CostEstimate(flops=10**9, bytes_accessed=10**7, transcendentals=0),
        name="travel",
    )(matrix, folded)


SLOTS = (((0,), 0), ((1, 4), 2), ((2,), 1), ((3, 6), 3), ((5,), 4), ((7,), 5))


def apply_kernel(
    m_ref, left_ref, right_ref, outer_ref, inner_ref, jc_ref, jr_ref, o_ref, raw, jc, jr, half_high, half_low, result,
    raw_sem, j_sem, out_sem,
):
    p = here()
    first_col, last_col = same(p.c, 0), same(p.c, GROUPS - 1)
    first_row, last_row = same(p.row, 0), same(p.row, 2 * GROUPS - 1)
    copies_j = [
        pltpu.make_async_copy(jr_ref, jr, j_sem.at[0]),
        pltpu.make_async_copy(jc_ref, jc, j_sem.at[1]),
    ]
    for copy in copies_j:
        copy.start()
    low, middle, high = pl.ds(0, PAIR), pl.ds(PAIR, COLS), pl.ds(PAIR + COLS, PAIR)

    def own_rows(s, pair, cond):
        rows = pl.ds(pair * PAIR, PAIR)
        when(cond, pltpu.make_async_copy(m_ref.at[rows], raw.at[s, :, middle], raw_sem.at[s, 0]).start)
        when(cond * (1 - first_col), pltpu.make_async_copy(left_ref.at[rows], raw.at[s, :, low], raw_sem.at[s, 1]).start)
        when(cond * (1 - last_col), pltpu.make_async_copy(right_ref.at[rows], raw.at[s, :, high], raw_sem.at[s, 2]).start)
        when(
            cond * first_col,
            pltpu.make_async_copy(m_ref.at[rows, pl.ds(0, PAIR)], raw.at[s, :, low], raw_sem.at[s, 1]).start,
        )
        when(
            cond * last_col,
            pltpu.make_async_copy(m_ref.at[rows, pl.ds(COLS - PAIR, PAIR)], raw.at[s, :, high], raw_sem.at[s, 2]).start,
        )

    def sent_rows(s, ref, cond):
        when(cond, pltpu.make_async_copy(ref.at[:, middle], raw.at[s, :, middle], raw_sem.at[s, 0]).start)
        when(cond * (1 - first_col), pltpu.make_async_copy(ref.at[:, low], raw.at[s, :, low], raw_sem.at[s, 1]).start)
        when(cond * (1 - last_col), pltpu.make_async_copy(ref.at[:, high], raw.at[s, :, high], raw_sem.at[s, 2]).start)
        when(
            cond * first_col,
            pltpu.make_async_copy(ref.at[:, pl.ds(PAIR, PAIR)], raw.at[s, :, low], raw_sem.at[s, 1]).start,
        )
        when(
            cond * last_col,
            pltpu.make_async_copy(ref.at[:, pl.ds(COLS, PAIR)], raw.at[s, :, high], raw_sem.at[s, 2]).start,
        )

    own_rows(1, 1, 1)
    own_rows(2, 0, 1)
    own_rows(0, 0, first_row)
    sent_rows(0, outer_ref, (1 - p.k) * (1 - first_row))
    sent_rows(0, inner_ref, p.k)
    own_rows(3, 1, last_row)
    sent_rows(3, outer_ref, p.k * (1 - last_row))
    sent_rows(3, inner_ref, 1 - p.k)
    copies_j[0].wait()
    for s in (1, 2, 0, 3):
        pltpu.make_async_copy(raw.at[s, :, middle], raw.at[s, :, middle], raw_sem.at[s, 0]).wait()
        pltpu.make_async_copy(raw.at[s, :, low], raw.at[s, :, low], raw_sem.at[s, 1]).wait()
        pltpu.make_async_copy(raw.at[s, :, high], raw.at[s, :, high], raw_sem.at[s, 2]).wait()
        turned = product(split(jr[s]), split(raw[s]))
        turned_high, turned_low = split(turned)
        half_high[s * BLK : (s + 1) * BLK] = turned_high
        half_low[s * BLK : (s + 1) * BLK] = turned_low
    copies_j[1].wait()
    stores = []
    for slots, panel in SLOTS:
        columns = pl.ds(panel * PAIR, PAIR)
        rotation = jc[slots[0]] if len(slots) == 1 else jnp.concatenate([jc[slots[0]], jc[slots[1]]], axis=1)
        turned = product((half_high[:, columns], half_low[:, columns]), split(rotation))
        for n, slot in enumerate(slots):
            result[slot] = turned[:, n * BLK : (n + 1) * BLK]
            store = pltpu.make_async_copy(result.at[slot], o_ref.at[:, pl.ds(slot * BLK, BLK)], out_sem.at[slot])
            store.start()
            stores.append(store)
    for store in stores:
        store.wait()


def apply(matrix, parts):
    any_spec = pl.BlockSpec(memory_space=pltpu.HBM)
    return pl.pallas_call(
        apply_kernel,
        out_shape=jax.ShapeDtypeStruct((ROWS, COLS), F32),
        in_specs=[any_spec] * 7,
        out_specs=any_spec,
        scratch_shapes=[
            pltpu.VMEM((4, PAIR, WIDE), F32),
            pltpu.VMEM((8, PAIR, BLK), F32),
            pltpu.VMEM((4, BLK, PAIR), F32),
            pltpu.VMEM((ROWS, WIDE), BF16),
            pltpu.VMEM((ROWS, WIDE), BF16),
            pltpu.VMEM((8, ROWS, BLK), F32),
            pltpu.SemaphoreType.DMA((4, 3)),
            pltpu.SemaphoreType.DMA((2,)),
            pltpu.SemaphoreType.DMA((8,)),
        ],
        compiler_params=pltpu.CompilerParams(vmem_limit_bytes=48 * MIB),
        cost_estimate=pl.CostEstimate(flops=2 * 10**9, bytes_accessed=10**7, transcendentals=0),
        name="apply",
    )(matrix, *parts)


def local(matrix):
    return apply(matrix, travel(matrix, first(matrix)))


def solution(mesh):
    spec = P("row", "col")
    return jax.shard_map(local, mesh=mesh, in_specs=(spec,), out_specs=spec, check_vma=False)
```

```python
import math

import jax
import jax.numpy as jnp
from jax import lax
from jax.experimental import pallas as pl
from jax.experimental.pallas import tpu as pltpu
from jax.sharding import PartitionSpec as P

MESH = pl.DeviceIdType.MESH
F32 = jnp.float32
BF16 = jnp.bfloat16
BLK = 128
PAIR = 256
INNER = 4
ROWS = 512
COLS = 1024
WIDE = COLS + 2 * PAIR
GROUPS = 16
FOLD = 264


def split(value):
    high = value.astype(BF16)
    return high, (value - high.astype(F32)).astype(BF16)


def product(first, second):
    (first_high, first_low), (second_high, second_low) = first, second
    left = jnp.concatenate([first_high, first_high, first_low], axis=1)
    right = jnp.concatenate([second_high, second_low, second_high], axis=0)
    return jnp.dot(left, right, preferred_element_type=F32)


def pair_rotation(square):
    i = lax.broadcasted_iota(jnp.int32, (PAIR, PAIR), 0)
    j = lax.broadcasted_iota(jnp.int32, (PAIR, PAIR), 1)
    weights = (j - i).astype(F32) * (0.25 / math.sqrt(PAIR) / (PAIR - 1))
    identity = jnp.where(i == j, 1.0, 0.0).astype(F32)
    current = square
    rotation = None
    for inner_step in range(INNER):
        last = inner_step == INNER - 1
        bracket = current * weights
        bracket_s = split(bracket)
        power = product(bracket_s, bracket_s)
        power_s = split(power)
        if not last:
            half = current + product(split(current), bracket_s)
        if rotation is None:
            turned = identity + bracket
        else:
            turned = rotation + product(split(rotation), bracket_s)
        power2 = product(power_s, power_s)
        if not last:
            both = half - product(bracket_s, split(half))
        series = 0.375 * identity + 0.3125 * power + 0.0625 * power2
        polish = split(0.5 * power + product(split(power2), split(series)))
        rotation = turned + product(split(turned), polish)
        if not last:
            half = both + product(split(both), polish)
            current = half + product(polish, split(half))
    return rotation


def fold(square):
    i = lax.broadcasted_iota(jnp.int32, (BLK, BLK), 0)
    j = lax.broadcasted_iota(jnp.int32, (BLK, BLK), 1)
    first, second = square[:BLK, :BLK], square[BLK:, BLK:]
    diagonal = jnp.sum(jnp.where(i == j, second, 0.0), axis=0, keepdims=True)
    return jnp.concatenate(
        [square[:BLK, BLK:], jnp.where(i <= j, first, second), jnp.broadcast_to(diagonal, (8, BLK))], axis=0
    )


def unfold(folded):
    i = lax.broadcasted_iota(jnp.int32, (BLK, BLK), 0)
    j = lax.broadcasted_iota(jnp.int32, (BLK, BLK), 1)
    side = folded[:BLK]
    middle = folded[BLK : 2 * BLK]
    flipped = middle.T
    first = jnp.where(i <= j, middle, flipped)
    second = jnp.where(i > j, middle, jnp.where(i < j, flipped, folded[2 * BLK : 2 * BLK + 1]))
    return jnp.concatenate(
        [jnp.concatenate([first, side], axis=1), jnp.concatenate([side.T, second], axis=1)], axis=0
    )


def choose(cond, yes, no):
    return cond * yes + (1 - cond) * no


def same(a, b):
    return int(a == b) if isinstance(a - b, int) else jnp.where(a == b, 1, 0)


def slot_of(group, member, half):
    step, slot = 0, 0
    for m, h, slot_in, step_in in (
        (0, 0, 2, 0), (1, 0, 4, 0), (2, 0, 6, 0), (3, 0, 0, 1),
        (0, 1, 7, -1), (1, 1, 1, 0), (2, 1, 3, 0), (3, 1, 5, 0),
    ):
        if h == half:
            slot = slot + same(member, m) * slot_in
            step = step + same(member, m) * step_in
    first, last = same(group, 0), same(group, GROUPS - 1)
    if half == 0:
        slot = slot - first * same(member, 0) * 2 + last * same(member, 3) * 7
        step = step - last * same(member, 3)
    else:
        slot = slot - first * same(member, 0) * 5
        step = step + first * same(member, 0)
    return step, slot


def maker_of(group, slot):
    step, member = {0: (-1, 3), 1: (0, 1), 2: (0, 0), 3: (0, 2), 4: (0, 1), 5: (0, 3), 6: (0, 2), 7: (1, 0)}[slot]
    if slot == 0:
        return choose(same(group, 0), 0, step), choose(same(group, 0), 0, member)
    if slot == 7:
        return choose(same(group, GROUPS - 1), 0, step), choose(same(group, GROUPS - 1), 3, member)
    return step, member


class Place:
    def __init__(self, row, col):
        self.row, self.c = row, col
        self.k, self.R = row % 2, row // 2
        self.x, self.zh = self.R % 4, self.R // 4
        self.y, self.zl = self.c % 4, self.c // 4
        self.on_diagonal = same(self.R, self.c)
        self.in_relay = same(self.zh, self.zl)

    def at(self, k=None, x=None, zh=None, y=None, zl=None):
        k = self.k if k is None else k
        x = self.x if x is None else x
        zh = self.zh if zh is None else zh
        y = self.y if y is None else y
        zl = self.zl if zl is None else zl
        return (2 * (4 * zh + x) + k, 4 * zl + y)


def scatter_out(p):
    found = []
    for j in range(2):
        q = 2 * p.k + j
        own = (1 - p.k) * same(p.x, q)
        found.append((j, "col", p.on_diagonal * own, p.on_diagonal * (1 - own), p.at(k=0, x=q)))
        own = p.k * same(p.y, q)
        found.append((j, "row", p.on_diagonal * own, p.on_diagonal * (1 - own), p.at(k=1, y=q)))
    return found


def cross_out(p):
    found = []
    for t in (2, 1, 3):
        row = choose(p.k, p.row, p.at(zh=(p.zh + t) % 4)[0])
        col = choose(p.k, p.at(zl=(p.zl + t) % 4)[1], p.c)
        found.append((p.in_relay, (row, col)))
    return found


def spread_out(p):
    found = []
    for half in range(2):
        step, slot = slot_of(p.c, p.x, half)
        core, stays = slot % 2, same(step, 0)
        found.append(("col", half, 0, (1 - p.k) * (1 - stays), (2 * p.R + core, p.c + step), slot))
        for t in (2, 1, 3, 0):
            own = 1 - core if t == 0 else 0
            device = p.at(k=core, x=(p.x + t) % 4)
            found.append(("col", half, (1 - p.k) * stays * own, (1 - p.k) * stays * (1 - own), device, slot))
        step, slot = slot_of(p.R, p.y, half)
        core, stays = slot // 4, same(step, 0)
        found.append(("row", half, 0, p.k * (1 - stays), (2 * (p.R + step) + core, p.c), slot % 4))
        for t in (2, 1, 3, 0):
            own = core if t == 0 else 0
            device = p.at(k=core, y=(p.y + t) % 4)
            found.append(("row", half, p.k * stays * own, p.k * stays * (1 - own), device, slot % 4))
    return found


def hub_out(p):
    first, last = same(p.c, 0), same(p.c, GROUPS - 1)
    cond = choose(p.k, same(p.x, 0) * (1 - last), same(p.x, 3) * (1 - first))
    found = [("col", cond, 7 * p.k, [p.at(x=(p.x + t) % 4) for t in (2, 1, 3)])]
    first, last = same(p.R, 0), same(p.R, GROUPS - 1)
    cond = choose(p.k, same(p.y, 0) * (1 - last), same(p.y, 3) * (1 - first))
    found.append(("row", cond, 3 * p.k, [p.at(y=(p.y + t) % 4) for t in (2, 1, 3)]))
    return found


def outer_out(p):
    forward = p.k
    here = choose(forward, 1 - same(p.R, GROUPS - 1), 1 - same(p.R, 0))
    own_x = choose(forward, 3, 0)
    edge = same(p.x, own_x)
    next_row = (2 * (p.R + 2 * forward - 1) + 1 - p.k + 32) % 32
    found = []
    for q in range(4):
        relayed = here * edge * (1 - same(own_x, q))
        row = choose(relayed, p.at(x=q)[0], next_row)
        found.append((q, relayed, here * (1 - relayed), (row, p.c)))
    return found


def relay_role(p):
    forward = p.k
    own_x = choose(forward, 3, 0)
    inside = choose(forward, 1 - same(p.zh, 3), 1 - same(p.zh, 0))
    cond = inside * (1 - same(p.x, own_x))
    to_zh = (p.zh + choose(forward, 1, 3)) % 4
    return cond, p.at(k=1 - p.k, x=3 - own_x, zh=to_zh), p.at(x=own_x)


def side_out(p):
    found = []
    for side in range(2):
        exists = 1 - same(p.c, 0 if side else GROUPS - 1)
        own_y = 0 if side else 3
        crosses = same(p.y, own_y)
        for q in range(4):
            relayed = 0 if q == own_y else exists * crosses
            col = p.c + 1 - 2 * side
            if q != own_y:
                col = choose(relayed, p.at(y=q)[1], col)
            found.append((side, q, relayed, exists * (1 - relayed), (p.row, col)))
    return found


def side_relay(p):
    found = []
    for side in range(2):
        own_y = 0 if side else 3
        cond = (1 - same(p.zl, 0 if side else 3)) * (1 - same(p.y, own_y))
        found.append((side, cond, p.at(y=3 - own_y, zl=(p.zl + (3 if side else 1)) % 4), p.at(y=own_y)))
    return found


def edges_out(p):
    found = cross_out(p)
    found += [(cond, device) for _, _, _, cond, device, _ in spread_out(p)]
    for _, cond, _, devices in hub_out(p):
        found += [(cond, device) for device in devices]
    for _, relayed, direct, device in outer_out(p):
        found.append((relayed + direct, device))
    cond, device, _ = relay_role(p)
    found.append((cond, device))
    found.append((1, p.at(k=1 - p.k)))
    found += [(relayed + direct, device) for _, _, relayed, direct, device in side_out(p)]
    found += [(cond, device) for _, cond, device, _ in side_relay(p)]
    return found


def first_edges_out(p):
    return [(cond, device) for _, _, _, cond, device in scatter_out(p)]


def first_edges_in(p):
    member, source_x, source_y = choose(p.k, p.y, p.x), choose(p.k, p.x, p.y), choose(p.k, p.x, p.y)
    own = p.on_diagonal * same(p.k, member // 2)
    return [(p.in_relay * (1 - own), p.at(k=member // 2, x=source_x, y=source_y))]


def edges_in(p):
    source = choose(p.k, p.row, p.at(zh=p.zl)[0]), choose(p.k, p.at(zl=p.zh)[1], p.c)
    found = [(1 - p.in_relay, source)]
    for n in range(4):
        step, member = maker_of(p.c, 2 * n)
        step1, member1 = maker_of(p.c, 2 * n + 1)
        step, member = choose(p.k, step1, step), choose(p.k, member1, member)
        stays, own = same(step, 0), same(member, p.x)
        core = choose(stays, 0, choose(own, 0, p.k))
        found.append((1 - stays * own * (1 - p.k), (2 * (4 * p.zh + member) + core, p.c + own * step)))
        step, member = maker_of(p.R, n)
        step1, member1 = maker_of(p.R, 4 + n)
        step, member = choose(p.k, step1, step), choose(p.k, member1, member)
        stays, own = same(step, 0), same(member, p.y)
        core = choose(stays, 1, choose(own, 1, p.k))
        found.append((1 - stays * own * p.k, (2 * (p.R + own * step) + core, 4 * p.zl + member)))
    forward = 1 - p.k
    here = choose(forward, 1 - same(p.R, 0), 1 - same(p.R, GROUPS - 1))
    edge = same(p.x, choose(forward, 0, 3))
    source_row = (2 * (p.R + 1 - 2 * forward) + 1 - p.k + 32) % 32
    source_zh = source_row // 8
    for q in range(4):
        row = choose(edge, 8 * source_zh + 2 * q + 1 - p.k, source_row)
        found.append((here, (row, p.c)))
    relay, _, start = relay_role(p)
    found.append((relay, start))
    found.append((1, p.at(k=1 - p.k)))
    for side, cond, _, source in side_relay(p):
        found.append((cond, source))
        own_y = 0 if side else 3
        exists, crosses = 1 - same(p.c, GROUPS - 1 if side else 0), same(p.y, 3 - own_y)
        for q in range(4):
            col = choose(crosses, p.at(y=q, zl=(p.zl + (1 if side else 3)) % 4)[1], p.c - 1 + 2 * side)
            found.append((exists, (p.row, col)))
    return found


def here():
    return Place(lax.axis_index("row"), lax.axis_index("col"))


def when(cond, action):
    if isinstance(cond, int):
        if cond:
            action()
    else:
        pl.when(cond == 1)(action)


class Sends:
    def __init__(self, sems):
        self.sems, self.pending = sems, []

    def start(self, cond, source, target, recv_sem, device):
        index = len(self.pending)

        def make():
            return pltpu.make_async_remote_copy(
                src_ref=source,
                dst_ref=target,
                send_sem=self.sems.at[index],
                recv_sem=recv_sem,
                device_id=device,
                device_id_type=MESH,
            )

        self.pending.append((cond, make))
        when(cond, lambda: make().start())

    def finish(self):
        for cond, make in self.pending:
            when(cond, lambda make=make: make().wait_send())


def arrived(ref, sem, cond=1):
    when(cond, lambda: pltpu.make_async_copy(ref, ref, sem).wait())


def greet(edges_in, edges_out):
    barrier = pltpu.get_barrier_semaphore()
    for cond, device in edges_in:
        when(
            cond,
            lambda device=device: pl.semaphore_signal(barrier, inc=1, device_id=device, device_id_type=MESH),
        )
    count = sum(cond for cond, _ in edges_out)
    pl.when(count > 0)(lambda: pl.semaphore_wait(barrier, count))


def first_kernel(m_ref, out_ref, square, folded, received, load_sem, send_sem, receive_sem):
    p = here()
    loads = []
    for j in range(2):
        column = pl.multiple_of(p.k * ROWS + j * PAIR, PAIR)
        loads.append(
            pltpu.make_async_copy(
                m_ref.at[pl.ds(j * PAIR, PAIR), pl.ds(column, PAIR)], square.at[j], load_sem.at[j]
            )
        )
        when(p.on_diagonal, loads[j].start)

    def fold_both():
        for j in range(2):
            loads[j].wait()
            folded[j] = fold(square[j])

    when(p.on_diagonal, fold_both)
    greet(first_edges_in(p), first_edges_out(p))
    sends = Sends(send_sem)
    for j, _, own, cond, device in scatter_out(p):
        sends.start(cond, folded.at[j], received, receive_sem.at[0], device)
        when(own, pltpu.make_async_copy(folded.at[j], received, receive_sem.at[0]).start)

    def keep():
        pltpu.make_async_copy(received, received, receive_sem.at[0]).wait()
        out_ref[...] = received[...]

    when(p.in_relay, keep)
    when(1 - p.in_relay, lambda: out_ref.__setitem__(..., jnp.zeros((FOLD, BLK), F32)))
    sends.finish()


def travel_kernel(
    m_ref, first_ref, left_ref, right_ref, outer_ref, inner_ref, jc_ref, jr_ref,
    solver_in, out_c, out_r, relay, side_pass,
    send_sem, solver_sem, jc_sem, jr_sem, side_sem, outer_sem, outer_side_sem, inner_sem, relay_sem, side_pass_sem,
):
    p = here()
    greet(edges_in(p), edges_out(p))
    sends = Sends(send_sem)
    mate = p.at(k=1 - p.k)
    before, after = (p.row, p.c - 1), (p.row, p.c + 1)
    has_before, has_after = 1 - same(p.c, 0), 1 - same(p.c, GROUPS - 1)
    low = pl.multiple_of(p.k * PAIR, PAIR)
    other = pl.multiple_of((1 - p.k) * PAIR, PAIR)

    for cond, device in cross_out(p):
        sends.start(cond, first_ref, solver_in, solver_sem.at[0], device)

    sides = (left_ref, right_ref)
    for side, q, relayed, direct, device in side_out(p):
        part = m_ref.at[pl.ds(q * BLK, BLK), pl.ds(0 if side else COLS - PAIR, PAIR)]
        if not isinstance(relayed, int):
            sends.start(relayed, part, side_pass.at[side], side_pass_sem.at[side], device)
        sends.start(direct, part, sides[side].at[pl.ds(q * BLK, BLK)], side_sem.at[side, q], device)
    sends.start(1, m_ref.at[pl.ds(other, PAIR)], inner_ref.at[:, pl.ds(PAIR, COLS)], inner_sem.at[0], mate)
    for q, relayed, direct, device in outer_out(p):
        part = m_ref.at[pl.ds(low, PAIR), pl.ds(q * PAIR, PAIR)]
        sends.start(relayed, part, relay, relay_sem.at[0], device)
        sends.start(direct, part, outer_ref.at[:, pl.ds(PAIR + q * PAIR, PAIR)], outer_sem.at[q], device)

    for side, cond, device, _ in side_relay(p):
        arrived(side_pass.at[side], side_pass_sem.at[side], cond)
        part = pl.ds(pl.multiple_of(p.y * BLK, BLK), BLK)
        sends.start(cond, side_pass.at[side], sides[side].at[part], side_sem.at[side, p.y], device)
    relaying, relay_to, _ = relay_role(p)
    arrived(relay, relay_sem.at[0], relaying)
    sends.start(
        relaying, relay, outer_ref.at[:, pl.ds(pl.multiple_of(PAIR + p.x * PAIR, PAIR), PAIR)], outer_sem.at[p.x], relay_to
    )

    arrived(solver_in, solver_sem.at[0], 1 - p.in_relay)
    rotation = pair_rotation(unfold(jnp.where(p.in_relay == 1, first_ref[...], solver_in[...])))

    def keep_columns():
        for half in range(2):
            out_c[half] = rotation[:, half * BLK : (half + 1) * BLK]

    def keep_rows():
        flipped = rotation.T
        for half in range(2):
            out_r[half] = flipped[half * BLK : (half + 1) * BLK]

    when(1 - p.k, keep_columns)
    when(p.k, keep_rows)
    for kind, half, own, cond, device, slot in spread_out(p):
        source, target, sem = (out_c, jc_ref, jc_sem) if kind == "col" else (out_r, jr_ref, jr_sem)
        sends.start(cond, source.at[half], target.at[slot], sem.at[slot], device)
        if not isinstance(own, int):
            when(own, pltpu.make_async_copy(source.at[half], target.at[slot], sem.at[slot]).start)

    has_outer = choose(p.k, 1 - same(p.R, GROUPS - 1), 1 - same(p.R, 0))
    sends_on = choose(p.k, 1 - same(p.x, 3), 1 - same(p.x, 0))
    (_, _, _, next_device), *_ = outer_out(p)
    ends = (pl.ds(0, PAIR), pl.ds(PAIR + COLS, PAIR))
    for side, exists, edge_y in ((0, has_before, 0), (1, has_after, 3)):
        for q in range(4):
            arrived(sides[side].at[pl.ds(q * BLK, BLK)], side_sem.at[side, q], exists)
        sends.start(
            exists, sides[side].at[pl.ds(other, PAIR)], inner_ref.at[:, ends[side]], inner_sem.at[1 + side], mate
        )
        sends.start(
            sends_on * exists * same(p.y, edge_y), sides[side].at[pl.ds(low, PAIR)], outer_ref.at[:, ends[side]],
            outer_side_sem.at[side], next_device,
        )

    def outer_corners(cond):
        for q in range(4):
            arrived(outer_ref.at[:, pl.ds(PAIR + q * PAIR, PAIR)], outer_sem.at[q], cond * has_outer)
            if q == 0:
                sends.start(
                    cond * has_outer * has_before * (1 - sends_on * same(p.y, 0)), outer_ref.at[:, pl.ds(PAIR, PAIR)],
                    outer_ref.at[:, ends[1]], outer_side_sem.at[1], before,
                )
        sends.start(
            cond * has_outer * has_after * (1 - sends_on * same(p.y, 3)), outer_ref.at[:, pl.ds(COLS, PAIR)],
            outer_ref.at[:, ends[0]], outer_side_sem.at[0], after,
        )

    outer_corners(sends_on)
    (_, hub, _, _), (_, hub_r, _, _) = hub_out(p)
    for kind, cond, slot, devices in hub_out(p):
        target, sem = (jc_ref, jc_sem) if kind == "col" else (jr_ref, jr_sem)
        arrived(target.at[slot], sem.at[slot], cond)
        for device in devices:
            sends.start(cond, target.at[slot], target.at[slot], sem.at[slot], device)

    outer_corners(1 - sends_on)

    for n in (1, 2, 3, 0):
        slot = choose(p.k, (1, 3, 5, 7)[n - 1], 2 * n)
        arrived(jc_ref.at[slot], jc_sem.at[slot], 1 - hub * same(slot, 7 * p.k))
        sends.start(1, jc_ref.at[slot], jc_ref.at[slot], jc_sem.at[slot], mate)
    for n in range(4):
        arrived(jc_ref.at[2 * n + 1 - p.k], jc_sem.at[2 * n + 1 - p.k])
        arrived(jr_ref.at[n], jr_sem.at[n], 1 - hub_r * same(n, 3 * p.k))

    arrived(inner_ref.at[:, pl.ds(PAIR, COLS)], inner_sem.at[0])
    arrived(inner_ref.at[:, pl.ds(0, PAIR)], inner_sem.at[1], has_before)
    arrived(inner_ref.at[:, pl.ds(PAIR + COLS, PAIR)], inner_sem.at[2], has_after)
    arrived(outer_ref.at[:, pl.ds(0, PAIR)], outer_side_sem.at[0], has_outer * has_before)
    arrived(outer_ref.at[:, pl.ds(PAIR + COLS, PAIR)], outer_side_sem.at[1], has_outer * has_after)
    sends.finish()


MIB = 1024 * 1024


def first(matrix):
    return pl.pallas_call(
        first_kernel,
        out_shape=pltpu.VMEM((FOLD, BLK), F32),
        in_specs=[pl.BlockSpec(memory_space=pltpu.HBM)],
        out_specs=pl.BlockSpec(memory_space=pltpu.VMEM),
        scratch_shapes=[
            pltpu.VMEM((2, PAIR, PAIR), F32),
            pltpu.VMEM((2, FOLD, BLK), F32),
            pltpu.VMEM((FOLD, BLK), F32),
            pltpu.SemaphoreType.DMA((2,)),
            pltpu.SemaphoreType.DMA((4,)),
            pltpu.SemaphoreType.DMA((1,)),
        ],
        compiler_params=pltpu.CompilerParams(collective_id=0, has_side_effects=True, vmem_limit_bytes=62 * MIB),
        cost_estimate=pl.CostEstimate(flops=10**6, bytes_accessed=10**6, transcendentals=0),
        name="first",
    )(matrix)


def travel(matrix, folded):
    any_spec = pl.BlockSpec(memory_space=pl.ANY)
    shapes = [(ROWS, PAIR), (ROWS, PAIR), (PAIR, WIDE), (PAIR, WIDE), (8, PAIR, BLK), (4, BLK, PAIR)]
    return pl.pallas_call(
        travel_kernel,
        out_shape=[pltpu.VMEM(shape, F32) for shape in shapes],
        in_specs=[pl.BlockSpec(memory_space=pltpu.HBM), pl.BlockSpec(memory_space=pltpu.VMEM)],
        out_specs=[any_spec] * len(shapes),
        scratch_shapes=[
            pltpu.VMEM((FOLD, BLK), F32),
            pltpu.VMEM((2, PAIR, BLK), F32),
            pltpu.VMEM((2, BLK, PAIR), F32),
            pltpu.VMEM((PAIR, PAIR), F32),
            pltpu.VMEM((2, BLK, PAIR), F32),
            pltpu.SemaphoreType.DMA((112,)),
            pltpu.SemaphoreType.DMA((1,)),
            pltpu.SemaphoreType.DMA((8,)),
            pltpu.SemaphoreType.DMA((4,)),
            pltpu.SemaphoreType.DMA((2, 4)),
            pltpu.SemaphoreType.DMA((4,)),
            pltpu.SemaphoreType.DMA((2,)),
            pltpu.SemaphoreType.DMA((3,)),
            pltpu.SemaphoreType.DMA((1,)),
            pltpu.SemaphoreType.DMA((2,)),
        ],
        compiler_params=pltpu.CompilerParams(collective_id=1, has_side_effects=True, vmem_limit_bytes=32 * MIB),
        cost_estimate=pl.CostEstimate(flops=10**9, bytes_accessed=10**7, transcendentals=0),
        name="travel",
    )(matrix, folded)


SLOTS = (((0,), 0), ((1, 4), 2), ((2,), 1), ((3, 6), 3), ((5,), 4), ((7,), 5))


def apply_kernel(
    m_ref, left_ref, right_ref, outer_ref, inner_ref, jc_ref, jr_ref, o_ref, raw, jc, jr, half_high, half_low, result,
    raw_sem, j_sem, out_sem,
):
    p = here()
    first_col, last_col = same(p.c, 0), same(p.c, GROUPS - 1)
    first_row, last_row = same(p.row, 0), same(p.row, 2 * GROUPS - 1)
    copies_j = [
        pltpu.make_async_copy(jr_ref, jr, j_sem.at[0]),
        pltpu.make_async_copy(jc_ref, jc, j_sem.at[1]),
    ]
    for copy in copies_j:
        copy.start()
    low, middle, high = pl.ds(0, PAIR), pl.ds(PAIR, COLS), pl.ds(PAIR + COLS, PAIR)

    def own_rows(s, pair, cond):
        rows = pl.ds(pair * PAIR, PAIR)
        when(cond, pltpu.make_async_copy(m_ref.at[rows], raw.at[s, :, middle], raw_sem.at[s, 0]).start)
        when(cond * (1 - first_col), pltpu.make_async_copy(left_ref.at[rows], raw.at[s, :, low], raw_sem.at[s, 1]).start)
        when(cond * (1 - last_col), pltpu.make_async_copy(right_ref.at[rows], raw.at[s, :, high], raw_sem.at[s, 2]).start)
        when(
            cond * first_col,
            pltpu.make_async_copy(m_ref.at[rows, pl.ds(0, PAIR)], raw.at[s, :, low], raw_sem.at[s, 1]).start,
        )
        when(
            cond * last_col,
            pltpu.make_async_copy(m_ref.at[rows, pl.ds(COLS - PAIR, PAIR)], raw.at[s, :, high], raw_sem.at[s, 2]).start,
        )

    def sent_rows(s, ref, cond):
        when(cond, pltpu.make_async_copy(ref.at[:, middle], raw.at[s, :, middle], raw_sem.at[s, 0]).start)
        when(cond * (1 - first_col), pltpu.make_async_copy(ref.at[:, low], raw.at[s, :, low], raw_sem.at[s, 1]).start)
        when(cond * (1 - last_col), pltpu.make_async_copy(ref.at[:, high], raw.at[s, :, high], raw_sem.at[s, 2]).start)
        when(
            cond * first_col,
            pltpu.make_async_copy(ref.at[:, pl.ds(PAIR, PAIR)], raw.at[s, :, low], raw_sem.at[s, 1]).start,
        )
        when(
            cond * last_col,
            pltpu.make_async_copy(ref.at[:, pl.ds(COLS, PAIR)], raw.at[s, :, high], raw_sem.at[s, 2]).start,
        )

    own_rows(1, 1, 1)
    own_rows(2, 0, 1)
    own_rows(0, 0, first_row)
    sent_rows(0, outer_ref, (1 - p.k) * (1 - first_row))
    sent_rows(0, inner_ref, p.k)
    own_rows(3, 1, last_row)
    sent_rows(3, outer_ref, p.k * (1 - last_row))
    sent_rows(3, inner_ref, 1 - p.k)
    copies_j[0].wait()
    for s in (1, 2, 0, 3):
        pltpu.make_async_copy(raw.at[s, :, middle], raw.at[s, :, middle], raw_sem.at[s, 0]).wait()
        pltpu.make_async_copy(raw.at[s, :, low], raw.at[s, :, low], raw_sem.at[s, 1]).wait()
        pltpu.make_async_copy(raw.at[s, :, high], raw.at[s, :, high], raw_sem.at[s, 2]).wait()
        (high_j, low_j), (high_m, low_m) = split(jr[s]), split(raw[s])
        both = jnp.dot(jnp.concatenate([high_j, low_j], axis=0), high_m, preferred_element_type=F32)
        turned = both[:BLK] + both[BLK:] + jnp.dot(high_j, low_m, preferred_element_type=F32)
        turned_high, turned_low = split(turned)
        half_high[s * BLK : (s + 1) * BLK] = turned_high
        half_low[s * BLK : (s + 1) * BLK] = turned_low
    copies_j[1].wait()
    stores = []
    for slots, panel in SLOTS:
        columns = pl.ds(panel * PAIR, PAIR)
        if len(slots) == 1:
            high_j, low_j = split(jc[slots[0]])
            both = jnp.dot(
                half_high[:, columns], jnp.concatenate([high_j, low_j], axis=1), preferred_element_type=F32
            )
            turned = both[:, :BLK] + both[:, BLK:] + jnp.dot(half_low[:, columns], high_j, preferred_element_type=F32)
        else:
            rotation = jnp.concatenate([jc[slots[0]], jc[slots[1]]], axis=1)
            turned = product((half_high[:, columns], half_low[:, columns]), split(rotation))
        for n, slot in enumerate(slots):
            result[slot] = turned[:, n * BLK : (n + 1) * BLK]
            store = pltpu.make_async_copy(result.at[slot], o_ref.at[:, pl.ds(slot * BLK, BLK)], out_sem.at[slot])
            store.start()
            stores.append(store)
    for store in stores:
        store.wait()


def apply(matrix, parts):
    any_spec = pl.BlockSpec(memory_space=pltpu.HBM)
    return pl.pallas_call(
        apply_kernel,
        out_shape=jax.ShapeDtypeStruct((ROWS, COLS), F32),
        in_specs=[any_spec] * 7,
        out_specs=any_spec,
        scratch_shapes=[
            pltpu.VMEM((4, PAIR, WIDE), F32),
            pltpu.VMEM((8, PAIR, BLK), F32),
            pltpu.VMEM((4, BLK, PAIR), F32),
            pltpu.VMEM((ROWS, WIDE), BF16),
            pltpu.VMEM((ROWS, WIDE), BF16),
            pltpu.VMEM((8, ROWS, BLK), F32),
            pltpu.SemaphoreType.DMA((4, 3)),
            pltpu.SemaphoreType.DMA((2,)),
            pltpu.SemaphoreType.DMA((8,)),
        ],
        compiler_params=pltpu.CompilerParams(vmem_limit_bytes=48 * MIB),
        cost_estimate=pl.CostEstimate(flops=2 * 10**9, bytes_accessed=10**7, transcendentals=0),
        name="apply",
    )(matrix, *parts)


def local(matrix):
    matrix = pltpu.with_memory_space_constraint(matrix, pltpu.HBM)
    return apply(matrix, travel(matrix, first(matrix)))


def solution(mesh):
    spec = P("row", "col")
    return jax.shard_map(local, mesh=mesh, in_specs=(spec,), out_specs=spec, check_vma=False)
```

```python
import math

import jax
import jax.numpy as jnp
from jax import lax
from jax.experimental import pallas as pl
from jax.experimental.pallas import tpu as pltpu
from jax.sharding import PartitionSpec as P

MESH = pl.DeviceIdType.MESH
F32 = jnp.float32
BF16 = jnp.bfloat16
BLK = 128
PAIR = 256
INNER = 4
ROWS = 512
COLS = 1024
WIDE = COLS + 2 * PAIR
GROUPS = 16
FOLD = 264


def split(value):
    high = value.astype(BF16)
    return high, (value - high.astype(F32)).astype(BF16)


def product(first, second):
    (first_high, first_low), (second_high, second_low) = first, second
    left = jnp.concatenate([first_high, first_high, first_low], axis=1)
    right = jnp.concatenate([second_high, second_low, second_high], axis=0)
    return jnp.dot(left, right, preferred_element_type=F32)


def pair_rotation(square):
    i = lax.broadcasted_iota(jnp.int32, (PAIR, PAIR), 0)
    j = lax.broadcasted_iota(jnp.int32, (PAIR, PAIR), 1)
    weights = (j - i).astype(F32) * (0.25 / math.sqrt(PAIR) / (PAIR - 1))
    identity = jnp.where(i == j, 1.0, 0.0).astype(F32)
    current = square
    rotation = None
    for inner_step in range(INNER):
        last = inner_step == INNER - 1
        bracket = current * weights
        bracket_s = split(bracket)
        power = product(bracket_s, bracket_s)
        power_s = split(power)
        if not last:
            half = current + product(split(current), bracket_s)
        if rotation is None:
            turned = identity + bracket
        else:
            turned = rotation + product(split(rotation), bracket_s)
        power2 = product(power_s, power_s)
        if not last:
            both = half - product(bracket_s, split(half))
        series = 0.375 * identity + 0.3125 * power + 0.0625 * power2
        polish = split(0.5 * power + product(split(power2), split(series)))
        rotation = turned + product(split(turned), polish)
        if not last:
            half = both + product(split(both), polish)
            current = half + product(polish, split(half))
    return rotation


def fold(square):
    i = lax.broadcasted_iota(jnp.int32, (BLK, BLK), 0)
    j = lax.broadcasted_iota(jnp.int32, (BLK, BLK), 1)
    first, second = square[:BLK, :BLK], square[BLK:, BLK:]
    diagonal = jnp.sum(jnp.where(i == j, second, 0.0), axis=0, keepdims=True)
    return jnp.concatenate(
        [square[:BLK, BLK:], jnp.where(i <= j, first, second), jnp.broadcast_to(diagonal, (8, BLK))], axis=0
    )


def unfold(folded):
    i = lax.broadcasted_iota(jnp.int32, (BLK, BLK), 0)
    j = lax.broadcasted_iota(jnp.int32, (BLK, BLK), 1)
    side = folded[:BLK]
    middle = folded[BLK : 2 * BLK]
    flipped = middle.T
    first = jnp.where(i <= j, middle, flipped)
    second = jnp.where(i > j, middle, jnp.where(i < j, flipped, folded[2 * BLK : 2 * BLK + 1]))
    return jnp.concatenate(
        [jnp.concatenate([first, side], axis=1), jnp.concatenate([side.T, second], axis=1)], axis=0
    )


def choose(cond, yes, no):
    return cond * yes + (1 - cond) * no


def same(a, b):
    return int(a == b) if isinstance(a - b, int) else jnp.where(a == b, 1, 0)


def slot_of(group, member, half):
    step, slot = 0, 0
    for m, h, slot_in, step_in in (
        (0, 0, 2, 0), (1, 0, 4, 0), (2, 0, 6, 0), (3, 0, 0, 1),
        (0, 1, 7, -1), (1, 1, 1, 0), (2, 1, 3, 0), (3, 1, 5, 0),
    ):
        if h == half:
            slot = slot + same(member, m) * slot_in
            step = step + same(member, m) * step_in
    first, last = same(group, 0), same(group, GROUPS - 1)
    if half == 0:
        slot = slot - first * same(member, 0) * 2 + last * same(member, 3) * 7
        step = step - last * same(member, 3)
    else:
        slot = slot - first * same(member, 0) * 5
        step = step + first * same(member, 0)
    return step, slot


def maker_of(group, slot):
    step, member = {0: (-1, 3), 1: (0, 1), 2: (0, 0), 3: (0, 2), 4: (0, 1), 5: (0, 3), 6: (0, 2), 7: (1, 0)}[slot]
    if slot == 0:
        return choose(same(group, 0), 0, step), choose(same(group, 0), 0, member)
    if slot == 7:
        return choose(same(group, GROUPS - 1), 0, step), choose(same(group, GROUPS - 1), 3, member)
    return step, member


class Place:
    def __init__(self, row, col):
        self.row, self.c = row, col
        self.k, self.R = row % 2, row // 2
        self.x, self.zh = self.R % 4, self.R // 4
        self.y, self.zl = self.c % 4, self.c // 4
        self.on_diagonal = same(self.R, self.c)
        self.in_relay = same(self.zh, self.zl)

    def at(self, k=None, x=None, zh=None, y=None, zl=None):
        k = self.k if k is None else k
        x = self.x if x is None else x
        zh = self.zh if zh is None else zh
        y = self.y if y is None else y
        zl = self.zl if zl is None else zl
        return (2 * (4 * zh + x) + k, 4 * zl + y)


def scatter_out(p):
    found = []
    for j in range(2):
        q = 2 * p.k + j
        own = (1 - p.k) * same(p.x, q)
        found.append((j, "col", p.on_diagonal * own, p.on_diagonal * (1 - own), p.at(k=0, x=q)))
        own = p.k * same(p.y, q)
        found.append((j, "row", p.on_diagonal * own, p.on_diagonal * (1 - own), p.at(k=1, y=q)))
    return found


def cross_out(p):
    found = []
    for t in (2, 1, 3):
        row = choose(p.k, p.row, p.at(zh=(p.zh + t) % 4)[0])
        col = choose(p.k, p.at(zl=(p.zl + t) % 4)[1], p.c)
        found.append((p.in_relay, (row, col)))
    return found


def spread_out(p):
    found = []
    for half in range(2):
        step, slot = slot_of(p.c, p.x, half)
        core, stays = slot % 2, same(step, 0)
        found.append(("col", half, 0, (1 - p.k) * (1 - stays), (2 * p.R + core, p.c + step), slot))
        for t in (2, 1, 3, 0):
            own = 1 - core if t == 0 else 0
            device = p.at(k=core, x=(p.x + t) % 4)
            found.append(("col", half, (1 - p.k) * stays * own, (1 - p.k) * stays * (1 - own), device, slot))
        step, slot = slot_of(p.R, p.y, half)
        core, stays = slot // 4, same(step, 0)
        found.append(("row", half, 0, p.k * (1 - stays), (2 * (p.R + step) + core, p.c), slot % 4))
        for t in (2, 1, 3, 0):
            own = core if t == 0 else 0
            device = p.at(k=core, y=(p.y + t) % 4)
            found.append(("row", half, p.k * stays * own, p.k * stays * (1 - own), device, slot % 4))
    return found


def hub_out(p):
    first, last = same(p.c, 0), same(p.c, GROUPS - 1)
    cond = choose(p.k, same(p.x, 0) * (1 - last), same(p.x, 3) * (1 - first))
    found = [("col", cond, 7 * p.k, [p.at(x=(p.x + t) % 4) for t in (2, 1, 3)])]
    first, last = same(p.R, 0), same(p.R, GROUPS - 1)
    cond = choose(p.k, same(p.y, 0) * (1 - last), same(p.y, 3) * (1 - first))
    found.append(("row", cond, 3 * p.k, [p.at(y=(p.y + t) % 4) for t in (2, 1, 3)]))
    return found


def outer_out(p):
    forward = p.k
    here = choose(forward, 1 - same(p.R, GROUPS - 1), 1 - same(p.R, 0))
    own_x = choose(forward, 3, 0)
    edge = same(p.x, own_x)
    next_row = (2 * (p.R + 2 * forward - 1) + 1 - p.k + 32) % 32
    found = []
    for q in range(4):
        relayed = here * edge * (1 - same(own_x, q))
        row = choose(relayed, p.at(x=q)[0], next_row)
        found.append((q, relayed, here * (1 - relayed), (row, p.c)))
    return found


def relay_role(p):
    forward = p.k
    own_x = choose(forward, 3, 0)
    inside = choose(forward, 1 - same(p.zh, 3), 1 - same(p.zh, 0))
    cond = inside * (1 - same(p.x, own_x))
    to_zh = (p.zh + choose(forward, 1, 3)) % 4
    return cond, p.at(k=1 - p.k, x=3 - own_x, zh=to_zh), p.at(x=own_x)


def side_out(p):
    found = []
    for side in range(2):
        exists = 1 - same(p.c, 0 if side else GROUPS - 1)
        own_y = 0 if side else 3
        crosses = same(p.y, own_y)
        for q in range(4):
            relayed = 0 if q == own_y else exists * crosses
            col = p.c + 1 - 2 * side
            if q != own_y:
                col = choose(relayed, p.at(y=q)[1], col)
            found.append((side, q, relayed, exists * (1 - relayed), (p.row, col)))
    return found


def side_relay(p):
    found = []
    for side in range(2):
        own_y = 0 if side else 3
        cond = (1 - same(p.zl, 0 if side else 3)) * (1 - same(p.y, own_y))
        found.append((side, cond, p.at(y=3 - own_y, zl=(p.zl + (3 if side else 1)) % 4), p.at(y=own_y)))
    return found


def edges_out(p):
    found = cross_out(p)
    found += [(cond, device) for _, _, _, cond, device, _ in spread_out(p)]
    for _, cond, _, devices in hub_out(p):
        found += [(cond, device) for device in devices]
    for _, relayed, direct, device in outer_out(p):
        found.append((relayed + direct, device))
    cond, device, _ = relay_role(p)
    found.append((cond, device))
    found.append((1, p.at(k=1 - p.k)))
    found += [(relayed + direct, device) for _, _, relayed, direct, device in side_out(p)]
    found += [(cond, device) for _, cond, device, _ in side_relay(p)]
    return found


def first_edges_out(p):
    return [(cond, device) for _, _, _, cond, device in scatter_out(p)]


def first_edges_in(p):
    member, source_x, source_y = choose(p.k, p.y, p.x), choose(p.k, p.x, p.y), choose(p.k, p.x, p.y)
    own = p.on_diagonal * same(p.k, member // 2)
    return [(p.in_relay * (1 - own), p.at(k=member // 2, x=source_x, y=source_y))]


def edges_in(p):
    source = choose(p.k, p.row, p.at(zh=p.zl)[0]), choose(p.k, p.at(zl=p.zh)[1], p.c)
    found = [(1 - p.in_relay, source)]
    for n in range(4):
        step, member = maker_of(p.c, 2 * n)
        step1, member1 = maker_of(p.c, 2 * n + 1)
        step, member = choose(p.k, step1, step), choose(p.k, member1, member)
        stays, own = same(step, 0), same(member, p.x)
        core = choose(stays, 0, choose(own, 0, p.k))
        found.append((1 - stays * own * (1 - p.k), (2 * (4 * p.zh + member) + core, p.c + own * step)))
        step, member = maker_of(p.R, n)
        step1, member1 = maker_of(p.R, 4 + n)
        step, member = choose(p.k, step1, step), choose(p.k, member1, member)
        stays, own = same(step, 0), same(member, p.y)
        core = choose(stays, 1, choose(own, 1, p.k))
        found.append((1 - stays * own * p.k, (2 * (p.R + own * step) + core, 4 * p.zl + member)))
    forward = 1 - p.k
    here = choose(forward, 1 - same(p.R, 0), 1 - same(p.R, GROUPS - 1))
    edge = same(p.x, choose(forward, 0, 3))
    source_row = (2 * (p.R + 1 - 2 * forward) + 1 - p.k + 32) % 32
    source_zh = source_row // 8
    for q in range(4):
        row = choose(edge, 8 * source_zh + 2 * q + 1 - p.k, source_row)
        found.append((here, (row, p.c)))
    relay, _, start = relay_role(p)
    found.append((relay, start))
    found.append((1, p.at(k=1 - p.k)))
    for side, cond, _, source in side_relay(p):
        found.append((cond, source))
        own_y = 0 if side else 3
        exists, crosses = 1 - same(p.c, GROUPS - 1 if side else 0), same(p.y, 3 - own_y)
        for q in range(4):
            col = choose(crosses, p.at(y=q, zl=(p.zl + (1 if side else 3)) % 4)[1], p.c - 1 + 2 * side)
            found.append((exists, (p.row, col)))
    return found


def here():
    return Place(lax.axis_index("row"), lax.axis_index("col"))


def when(cond, action):
    if isinstance(cond, int):
        if cond:
            action()
    else:
        pl.when(cond == 1)(action)


class Sends:
    def __init__(self, sems):
        self.sems, self.pending = sems, []

    def start(self, cond, source, target, recv_sem, device):
        index = len(self.pending)

        def make():
            return pltpu.make_async_remote_copy(
                src_ref=source,
                dst_ref=target,
                send_sem=self.sems.at[index],
                recv_sem=recv_sem,
                device_id=device,
                device_id_type=MESH,
            )

        self.pending.append((cond, make))
        when(cond, lambda: make().start())

    def finish(self):
        for cond, make in self.pending:
            when(cond, lambda make=make: make().wait_send())


def arrived(ref, sem, cond=1):
    when(cond, lambda: pltpu.make_async_copy(ref, ref, sem).wait())


def greet(edges_in, edges_out):
    barrier = pltpu.get_barrier_semaphore()
    for cond, device in edges_in:
        when(
            cond,
            lambda device=device: pl.semaphore_signal(barrier, inc=1, device_id=device, device_id_type=MESH),
        )
    count = sum(cond for cond, _ in edges_out)
    pl.when(count > 0)(lambda: pl.semaphore_wait(barrier, count))


def first_kernel(m_ref, out_ref, square, folded, received, load_sem, send_sem, receive_sem):
    p = here()
    loads = []
    for j in range(2):
        column = pl.multiple_of(p.k * ROWS + j * PAIR, PAIR)
        loads.append(
            pltpu.make_async_copy(
                m_ref.at[pl.ds(j * PAIR, PAIR), pl.ds(column, PAIR)], square.at[j], load_sem.at[j]
            )
        )
        when(p.on_diagonal, loads[j].start)

    def fold_both():
        for j in range(2):
            loads[j].wait()
            folded[j] = fold(square[j])

    when(p.on_diagonal, fold_both)
    greet(first_edges_in(p), first_edges_out(p))
    sends = Sends(send_sem)
    for j, _, own, cond, device in scatter_out(p):
        sends.start(cond, folded.at[j], received, receive_sem.at[0], device)
        when(own, pltpu.make_async_copy(folded.at[j], received, receive_sem.at[0]).start)

    def keep():
        pltpu.make_async_copy(received, received, receive_sem.at[0]).wait()
        out_ref[...] = received[...]

    when(p.in_relay, keep)
    when(1 - p.in_relay, lambda: out_ref.__setitem__(..., jnp.zeros((FOLD, BLK), F32)))
    sends.finish()


def travel_kernel(
    m_ref, first_ref, left_ref, right_ref, outer_ref, inner_ref, jc_ref, jr_ref,
    solver_in, out_c, out_r, relay, side_pass,
    send_sem, solver_sem, jc_sem, jr_sem, side_sem, outer_sem, outer_side_sem, inner_sem, relay_sem, side_pass_sem,
):
    p = here()
    greet(edges_in(p), edges_out(p))
    sends = Sends(send_sem)
    mate = p.at(k=1 - p.k)
    before, after = (p.row, p.c - 1), (p.row, p.c + 1)
    has_before, has_after = 1 - same(p.c, 0), 1 - same(p.c, GROUPS - 1)
    low = pl.multiple_of(p.k * PAIR, PAIR)
    other = pl.multiple_of((1 - p.k) * PAIR, PAIR)

    for cond, device in cross_out(p):
        sends.start(cond, first_ref, solver_in, solver_sem.at[0], device)

    sides = (left_ref, right_ref)
    for side, q, relayed, direct, device in side_out(p):
        part = m_ref.at[pl.ds(q * BLK, BLK), pl.ds(0 if side else COLS - PAIR, PAIR)]
        if not isinstance(relayed, int):
            sends.start(relayed, part, side_pass.at[side], side_pass_sem.at[side], device)
        sends.start(direct, part, sides[side].at[pl.ds(q * BLK, BLK)], side_sem.at[side, q], device)
    sends.start(1, m_ref.at[pl.ds(other, PAIR)], inner_ref.at[:, pl.ds(PAIR, COLS)], inner_sem.at[0], mate)
    for q, relayed, direct, device in outer_out(p):
        part = m_ref.at[pl.ds(low, PAIR), pl.ds(q * PAIR, PAIR)]
        sends.start(relayed, part, relay, relay_sem.at[0], device)
        sends.start(direct, part, outer_ref.at[:, pl.ds(PAIR + q * PAIR, PAIR)], outer_sem.at[q], device)

    for side, cond, device, _ in side_relay(p):
        arrived(side_pass.at[side], side_pass_sem.at[side], cond)
        part = pl.ds(pl.multiple_of(p.y * BLK, BLK), BLK)
        sends.start(cond, side_pass.at[side], sides[side].at[part], side_sem.at[side, p.y], device)
    relaying, relay_to, _ = relay_role(p)
    arrived(relay, relay_sem.at[0], relaying)
    sends.start(
        relaying, relay, outer_ref.at[:, pl.ds(pl.multiple_of(PAIR + p.x * PAIR, PAIR), PAIR)], outer_sem.at[p.x], relay_to
    )

    arrived(solver_in, solver_sem.at[0], 1 - p.in_relay)
    rotation = pair_rotation(unfold(jnp.where(p.in_relay == 1, first_ref[...], solver_in[...])))

    def keep_columns():
        for half in range(2):
            out_c[half] = rotation[:, half * BLK : (half + 1) * BLK]

    def keep_rows():
        flipped = rotation.T
        for half in range(2):
            out_r[half] = flipped[half * BLK : (half + 1) * BLK]

    when(1 - p.k, keep_columns)
    when(p.k, keep_rows)
    for kind, half, own, cond, device, slot in spread_out(p):
        source, target, sem = (out_c, jc_ref, jc_sem) if kind == "col" else (out_r, jr_ref, jr_sem)
        sends.start(cond, source.at[half], target.at[slot], sem.at[slot], device)
        if not isinstance(own, int):
            when(own, pltpu.make_async_copy(source.at[half], target.at[slot], sem.at[slot]).start)

    has_outer = choose(p.k, 1 - same(p.R, GROUPS - 1), 1 - same(p.R, 0))
    sends_on = choose(p.k, 1 - same(p.x, 3), 1 - same(p.x, 0))
    (_, _, _, next_device), *_ = outer_out(p)
    ends = (pl.ds(0, PAIR), pl.ds(PAIR + COLS, PAIR))
    for side, exists, edge_y in ((0, has_before, 0), (1, has_after, 3)):
        for q in range(4):
            arrived(sides[side].at[pl.ds(q * BLK, BLK)], side_sem.at[side, q], exists)
        sends.start(
            exists, sides[side].at[pl.ds(other, PAIR)], inner_ref.at[:, ends[side]], inner_sem.at[1 + side], mate
        )
        sends.start(
            sends_on * exists * same(p.y, edge_y), sides[side].at[pl.ds(low, PAIR)], outer_ref.at[:, ends[side]],
            outer_side_sem.at[side], next_device,
        )

    def outer_corners(cond):
        for q in range(4):
            arrived(outer_ref.at[:, pl.ds(PAIR + q * PAIR, PAIR)], outer_sem.at[q], cond * has_outer)
            if q == 0:
                sends.start(
                    cond * has_outer * has_before * (1 - sends_on * same(p.y, 0)), outer_ref.at[:, pl.ds(PAIR, PAIR)],
                    outer_ref.at[:, ends[1]], outer_side_sem.at[1], before,
                )
        sends.start(
            cond * has_outer * has_after * (1 - sends_on * same(p.y, 3)), outer_ref.at[:, pl.ds(COLS, PAIR)],
            outer_ref.at[:, ends[0]], outer_side_sem.at[0], after,
        )

    outer_corners(sends_on)
    (_, hub, _, _), (_, hub_r, _, _) = hub_out(p)
    for kind, cond, slot, devices in hub_out(p):
        target, sem = (jc_ref, jc_sem) if kind == "col" else (jr_ref, jr_sem)
        arrived(target.at[slot], sem.at[slot], cond)
        for device in devices:
            sends.start(cond, target.at[slot], target.at[slot], sem.at[slot], device)

    outer_corners(1 - sends_on)

    for n in (1, 2, 3, 0):
        slot = choose(p.k, (1, 3, 5, 7)[n - 1], 2 * n)
        arrived(jc_ref.at[slot], jc_sem.at[slot], 1 - hub * same(slot, 7 * p.k))
        sends.start(1, jc_ref.at[slot], jc_ref.at[slot], jc_sem.at[slot], mate)
    for n in range(4):
        arrived(jc_ref.at[2 * n + 1 - p.k], jc_sem.at[2 * n + 1 - p.k])
        arrived(jr_ref.at[n], jr_sem.at[n], 1 - hub_r * same(n, 3 * p.k))

    arrived(inner_ref.at[:, pl.ds(PAIR, COLS)], inner_sem.at[0])
    arrived(inner_ref.at[:, pl.ds(0, PAIR)], inner_sem.at[1], has_before)
    arrived(inner_ref.at[:, pl.ds(PAIR + COLS, PAIR)], inner_sem.at[2], has_after)
    arrived(outer_ref.at[:, pl.ds(0, PAIR)], outer_side_sem.at[0], has_outer * has_before)
    arrived(outer_ref.at[:, pl.ds(PAIR + COLS, PAIR)], outer_side_sem.at[1], has_outer * has_after)
    sends.finish()


MIB = 1024 * 1024


def first(matrix):
    return pl.pallas_call(
        first_kernel,
        out_shape=pltpu.VMEM((FOLD, BLK), F32),
        in_specs=[pl.BlockSpec(memory_space=pltpu.HBM)],
        out_specs=pl.BlockSpec(memory_space=pltpu.VMEM),
        scratch_shapes=[
            pltpu.VMEM((2, PAIR, PAIR), F32),
            pltpu.VMEM((2, FOLD, BLK), F32),
            pltpu.VMEM((FOLD, BLK), F32),
            pltpu.SemaphoreType.DMA((2,)),
            pltpu.SemaphoreType.DMA((4,)),
            pltpu.SemaphoreType.DMA((1,)),
        ],
        compiler_params=pltpu.CompilerParams(collective_id=0, has_side_effects=True, vmem_limit_bytes=62 * MIB),
        cost_estimate=pl.CostEstimate(flops=10**6, bytes_accessed=10**6, transcendentals=0),
        name="first",
    )(matrix)


def travel(matrix, folded):
    any_spec = pl.BlockSpec(memory_space=pl.ANY)
    shapes = [(ROWS, PAIR), (ROWS, PAIR), (PAIR, WIDE), (PAIR, WIDE), (8, PAIR, BLK), (4, BLK, PAIR)]
    return pl.pallas_call(
        travel_kernel,
        out_shape=[pltpu.VMEM(shape, F32) for shape in shapes],
        in_specs=[pl.BlockSpec(memory_space=pltpu.HBM), pl.BlockSpec(memory_space=pltpu.VMEM)],
        out_specs=[any_spec] * len(shapes),
        scratch_shapes=[
            pltpu.VMEM((FOLD, BLK), F32),
            pltpu.VMEM((2, PAIR, BLK), F32),
            pltpu.VMEM((2, BLK, PAIR), F32),
            pltpu.VMEM((PAIR, PAIR), F32),
            pltpu.VMEM((2, BLK, PAIR), F32),
            pltpu.SemaphoreType.DMA((112,)),
            pltpu.SemaphoreType.DMA((1,)),
            pltpu.SemaphoreType.DMA((8,)),
            pltpu.SemaphoreType.DMA((4,)),
            pltpu.SemaphoreType.DMA((2, 4)),
            pltpu.SemaphoreType.DMA((4,)),
            pltpu.SemaphoreType.DMA((2,)),
            pltpu.SemaphoreType.DMA((3,)),
            pltpu.SemaphoreType.DMA((1,)),
            pltpu.SemaphoreType.DMA((2,)),
        ],
        compiler_params=pltpu.CompilerParams(collective_id=1, has_side_effects=True, vmem_limit_bytes=32 * MIB),
        cost_estimate=pl.CostEstimate(flops=10**9, bytes_accessed=10**7, transcendentals=0),
        name="travel",
    )(matrix, folded)


SLOTS = (((0,), 0), ((1, 4), 2), ((2,), 1), ((3, 6), 3), ((5,), 4), ((7,), 5))


def apply_kernel(
    m_ref, left_ref, right_ref, outer_ref, inner_ref, jc, jr, o_ref, own, half_high, half_low, result, own_sem, out_sem,
):
    p = here()
    first_row, last_row = same(p.row, 0), same(p.row, 2 * GROUPS - 1)
    loads = []
    for pair in (1, 0):
        rows = pl.ds(pair * PAIR, PAIR)
        loads.append(pltpu.make_async_copy(m_ref.at[rows], own.at[rows], own_sem.at[pair]))
        loads[-1].start()
    low, middle, high = pl.ds(0, PAIR), pl.ds(PAIR, COLS), pl.ds(PAIR + COLS, PAIR)

    def turn(s, parts):
        high_j, low_j = split(jr[s])
        stacked = jnp.concatenate([high_j, low_j], axis=0)
        for columns, part in parts:
            high_m, low_m = split(part())
            both = jnp.dot(stacked, high_m, preferred_element_type=F32)
            turned = both[:BLK] + both[BLK:] + jnp.dot(high_j, low_m, preferred_element_type=F32)
            turned_high, turned_low = split(turned)
            half_high[s * BLK : (s + 1) * BLK, columns] = turned_high
            half_low[s * BLK : (s + 1) * BLK, columns] = turned_low

    def own_rows(s, pair):
        rows = pl.ds(pair * PAIR, PAIR)
        turn(s, ((middle, lambda: own[rows]), (low, lambda: left_ref[rows]), (high, lambda: right_ref[rows])))

    def sent_rows(s, ref):
        turn(s, ((middle, lambda: ref[:, middle]), (low, lambda: ref[:, low]), (high, lambda: ref[:, high])))

    when((1 - p.k) * (1 - first_row), lambda: sent_rows(0, outer_ref))
    when(p.k, lambda: sent_rows(0, inner_ref))
    when(p.k * (1 - last_row), lambda: sent_rows(3, outer_ref))
    when(1 - p.k, lambda: sent_rows(3, inner_ref))
    for load in loads:
        load.wait()
    own_rows(1, 1)
    own_rows(2, 0)
    when(first_row, lambda: own_rows(0, 0))
    when(last_row, lambda: own_rows(3, 1))

    def repeat(target, source):
        half_high[:, target] = half_high[:, source]
        half_low[:, target] = half_low[:, source]

    when(same(p.c, 0), lambda: repeat(low, pl.ds(PAIR, PAIR)))
    when(same(p.c, GROUPS - 1), lambda: repeat(high, pl.ds(COLS, PAIR)))
    stores = []
    for slots, panel in SLOTS:
        columns = pl.ds(panel * PAIR, PAIR)
        if len(slots) == 1:
            high_j, low_j = split(jc[slots[0]])
            both = jnp.dot(
                half_high[:, columns], jnp.concatenate([high_j, low_j], axis=1), preferred_element_type=F32
            )
            turned = both[:, :BLK] + both[:, BLK:] + jnp.dot(half_low[:, columns], high_j, preferred_element_type=F32)
        else:
            rotation = jnp.concatenate([jc[slots[0]], jc[slots[1]]], axis=1)
            turned = product((half_high[:, columns], half_low[:, columns]), split(rotation))
        for n, slot in enumerate(slots):
            result[slot] = turned[:, n * BLK : (n + 1) * BLK]
            store = pltpu.make_async_copy(result.at[slot], o_ref.at[:, pl.ds(slot * BLK, BLK)], out_sem.at[slot])
            store.start()
            stores.append(store)
    for store in stores:
        store.wait()


def apply(matrix, parts):
    hbm = pl.BlockSpec(memory_space=pltpu.HBM)
    vmem = pl.BlockSpec(memory_space=pltpu.VMEM)
    return pl.pallas_call(
        apply_kernel,
        out_shape=jax.ShapeDtypeStruct((ROWS, COLS), F32),
        in_specs=[hbm] + [vmem] * 6,
        out_specs=pl.BlockSpec(memory_space=pl.ANY),
        scratch_shapes=[
            pltpu.VMEM((ROWS, COLS), F32),
            pltpu.VMEM((ROWS, WIDE), BF16),
            pltpu.VMEM((ROWS, WIDE), BF16),
            pltpu.VMEM((8, ROWS, BLK), F32),
            pltpu.SemaphoreType.DMA((2,)),
            pltpu.SemaphoreType.DMA((8,)),
        ],
        compiler_params=pltpu.CompilerParams(vmem_limit_bytes=48 * MIB),
        cost_estimate=pl.CostEstimate(flops=2 * 10**9, bytes_accessed=10**7, transcendentals=0),
        name="apply",
    )(matrix, *parts)


def local(matrix):
    matrix = pltpu.with_memory_space_constraint(matrix, pltpu.HBM)
    return apply(matrix, travel(matrix, first(matrix)))


def solution(mesh):
    spec = P("row", "col")
    return jax.shard_map(local, mesh=mesh, in_specs=(spec,), out_specs=spec, check_vma=False)
```

```python
import math

import jax
import jax.numpy as jnp
from jax import lax
from jax.experimental import pallas as pl
from jax.experimental.pallas import tpu as pltpu
from jax.sharding import PartitionSpec as P

MESH = pl.DeviceIdType.MESH
F32 = jnp.float32
BF16 = jnp.bfloat16
BLK = 128
PAIR = 256
INNER = 4
ROWS = 512
COLS = 1024
WIDE = COLS + 2 * PAIR
GROUPS = 16
FOLD = 264


def split(value):
    high = value.astype(BF16)
    return high, (value - high.astype(F32)).astype(BF16)


def product(first, second):
    (first_high, first_low), (second_high, second_low) = first, second
    left = jnp.concatenate([first_high, first_high, first_low], axis=1)
    right = jnp.concatenate([second_high, second_low, second_high], axis=0)
    return jnp.dot(left, right, preferred_element_type=F32)


def pair_rotation(square):
    i = lax.broadcasted_iota(jnp.int32, (PAIR, PAIR), 0)
    j = lax.broadcasted_iota(jnp.int32, (PAIR, PAIR), 1)
    weights = (j - i).astype(F32) * (0.25 / math.sqrt(PAIR) / (PAIR - 1))
    identity = jnp.where(i == j, 1.0, 0.0).astype(F32)
    current = square
    rotation = None
    for inner_step in range(INNER):
        last = inner_step == INNER - 1
        bracket = current * weights
        bracket_s = split(bracket)
        power = product(bracket_s, bracket_s)
        power_s = split(power)
        if not last:
            half = current + product(split(current), bracket_s)
        if rotation is None:
            turned = identity + bracket
        else:
            turned = rotation + product(split(rotation), bracket_s)
        power2 = product(power_s, power_s)
        if not last:
            both = half - product(bracket_s, split(half))
        series = 0.375 * identity + 0.3125 * power + 0.0625 * power2
        polish = split(0.5 * power + product(split(power2), split(series)))
        rotation = turned + product(split(turned), polish)
        if not last:
            half = both + product(split(both), polish)
            current = half + product(polish, split(half))
    return rotation


def fold(square):
    i = lax.broadcasted_iota(jnp.int32, (BLK, BLK), 0)
    j = lax.broadcasted_iota(jnp.int32, (BLK, BLK), 1)
    first, second = square[:BLK, :BLK], square[BLK:, BLK:]
    diagonal = jnp.sum(jnp.where(i == j, second, 0.0), axis=0, keepdims=True)
    return jnp.concatenate(
        [square[:BLK, BLK:], jnp.where(i <= j, first, second), jnp.broadcast_to(diagonal, (8, BLK))], axis=0
    )


def unfold(folded):
    i = lax.broadcasted_iota(jnp.int32, (BLK, BLK), 0)
    j = lax.broadcasted_iota(jnp.int32, (BLK, BLK), 1)
    side = folded[:BLK]
    middle = folded[BLK : 2 * BLK]
    flipped = middle.T
    first = jnp.where(i <= j, middle, flipped)
    second = jnp.where(i > j, middle, jnp.where(i < j, flipped, folded[2 * BLK : 2 * BLK + 1]))
    return jnp.concatenate(
        [jnp.concatenate([first, side], axis=1), jnp.concatenate([side.T, second], axis=1)], axis=0
    )


def choose(cond, yes, no):
    return cond * yes + (1 - cond) * no


def same(a, b):
    return int(a == b) if isinstance(a - b, int) else jnp.where(a == b, 1, 0)


def slot_of(group, member, half):
    step, slot = 0, 0
    for m, h, slot_in, step_in in (
        (0, 0, 2, 0), (1, 0, 4, 0), (2, 0, 6, 0), (3, 0, 0, 1),
        (0, 1, 7, -1), (1, 1, 1, 0), (2, 1, 3, 0), (3, 1, 5, 0),
    ):
        if h == half:
            slot = slot + same(member, m) * slot_in
            step = step + same(member, m) * step_in
    first, last = same(group, 0), same(group, GROUPS - 1)
    if half == 0:
        slot = slot - first * same(member, 0) * 2 + last * same(member, 3) * 7
        step = step - last * same(member, 3)
    else:
        slot = slot - first * same(member, 0) * 5
        step = step + first * same(member, 0)
    return step, slot


def maker_of(group, slot):
    step, member = {0: (-1, 3), 1: (0, 1), 2: (0, 0), 3: (0, 2), 4: (0, 1), 5: (0, 3), 6: (0, 2), 7: (1, 0)}[slot]
    if slot == 0:
        return choose(same(group, 0), 0, step), choose(same(group, 0), 0, member)
    if slot == 7:
        return choose(same(group, GROUPS - 1), 0, step), choose(same(group, GROUPS - 1), 3, member)
    return step, member


class Place:
    def __init__(self, row, col):
        self.row, self.c = row, col
        self.k, self.R = row % 2, row // 2
        self.x, self.zh = self.R % 4, self.R // 4
        self.y, self.zl = self.c % 4, self.c // 4
        self.on_diagonal = same(self.R, self.c)
        self.in_relay = same(self.zh, self.zl)

    def at(self, k=None, x=None, zh=None, y=None, zl=None):
        k = self.k if k is None else k
        x = self.x if x is None else x
        zh = self.zh if zh is None else zh
        y = self.y if y is None else y
        zl = self.zl if zl is None else zl
        return (2 * (4 * zh + x) + k, 4 * zl + y)


def scatter_out(p):
    found = []
    for j in range(2):
        q = 2 * p.k + j
        own = (1 - p.k) * same(p.x, q)
        found.append((j, "col", p.on_diagonal * own, p.on_diagonal * (1 - own), p.at(k=0, x=q)))
        own = p.k * same(p.y, q)
        found.append((j, "row", p.on_diagonal * own, p.on_diagonal * (1 - own), p.at(k=1, y=q)))
    return found


def cross_out(p):
    found = []
    for t in (2, 1, 3):
        row = choose(p.k, p.row, p.at(zh=(p.zh + t) % 4)[0])
        col = choose(p.k, p.at(zl=(p.zl + t) % 4)[1], p.c)
        found.append((p.in_relay, (row, col)))
    return found


def spread_out(p):
    found = []
    for half in range(2):
        step, slot = slot_of(p.c, p.x, half)
        core, stays = slot % 2, same(step, 0)
        found.append(("col", half, 0, (1 - p.k) * (1 - stays), (2 * p.R + core, p.c + step), slot))
        for t in (2, 1, 3, 0):
            own = 1 - core if t == 0 else 0
            device = p.at(k=core, x=(p.x + t) % 4)
            found.append(("col", half, (1 - p.k) * stays * own, (1 - p.k) * stays * (1 - own), device, slot))
        step, slot = slot_of(p.R, p.y, half)
        core, stays = slot // 4, same(step, 0)
        found.append(("row", half, 0, p.k * (1 - stays), (2 * (p.R + step) + core, p.c), slot % 4))
        for t in (2, 1, 3, 0):
            own = core if t == 0 else 0
            device = p.at(k=core, y=(p.y + t) % 4)
            found.append(("row", half, p.k * stays * own, p.k * stays * (1 - own), device, slot % 4))
    return found


def hub_out(p):
    first, last = same(p.c, 0), same(p.c, GROUPS - 1)
    cond = choose(p.k, same(p.x, 0) * (1 - last), same(p.x, 3) * (1 - first))
    found = [("col", cond, 7 * p.k, [p.at(x=(p.x + t) % 4) for t in (2, 1, 3)])]
    first, last = same(p.R, 0), same(p.R, GROUPS - 1)
    cond = choose(p.k, same(p.y, 0) * (1 - last), same(p.y, 3) * (1 - first))
    found.append(("row", cond, 3 * p.k, [p.at(y=(p.y + t) % 4) for t in (2, 1, 3)]))
    return found


def outer_out(p):
    forward = p.k
    here = choose(forward, 1 - same(p.R, GROUPS - 1), 1 - same(p.R, 0))
    own_x = choose(forward, 3, 0)
    edge = same(p.x, own_x)
    next_row = (2 * (p.R + 2 * forward - 1) + 1 - p.k + 32) % 32
    found = []
    for q in range(4):
        relayed = here * edge * (1 - same(own_x, q))
        row = choose(relayed, p.at(x=q)[0], next_row)
        found.append((q, relayed, here * (1 - relayed), (row, p.c)))
    return found


def relay_role(p):
    forward = p.k
    own_x = choose(forward, 3, 0)
    inside = choose(forward, 1 - same(p.zh, 3), 1 - same(p.zh, 0))
    cond = inside * (1 - same(p.x, own_x))
    to_zh = (p.zh + choose(forward, 1, 3)) % 4
    return cond, p.at(k=1 - p.k, x=3 - own_x, zh=to_zh), p.at(x=own_x)


def side_out(p):
    found = []
    for side in range(2):
        exists = 1 - same(p.c, 0 if side else GROUPS - 1)
        own_y = 0 if side else 3
        crosses = same(p.y, own_y)
        for q in range(4):
            relayed = 0 if q == own_y else exists * crosses
            col = p.c + 1 - 2 * side
            if q != own_y:
                col = choose(relayed, p.at(y=q)[1], col)
            found.append((side, q, relayed, exists * (1 - relayed), (p.row, col)))
    return found


def side_relay(p):
    found = []
    for side in range(2):
        own_y = 0 if side else 3
        cond = (1 - same(p.zl, 0 if side else 3)) * (1 - same(p.y, own_y))
        found.append((side, cond, p.at(y=3 - own_y, zl=(p.zl + (3 if side else 1)) % 4), p.at(y=own_y)))
    return found


def edges_out(p):
    found = cross_out(p)
    found += [(cond, device) for _, _, _, cond, device, _ in spread_out(p)]
    for _, cond, _, devices in hub_out(p):
        found += [(cond, device) for device in devices]
    for _, relayed, direct, device in outer_out(p):
        found.append((relayed + direct, device))
    cond, device, _ = relay_role(p)
    found.append((cond, device))
    found.append((1, p.at(k=1 - p.k)))
    found += [(relayed + direct, device) for _, _, relayed, direct, device in side_out(p)]
    found += [(cond, device) for _, cond, device, _ in side_relay(p)]
    return found


def first_edges_out(p):
    return [(cond, device) for _, _, _, cond, device in scatter_out(p)]


def first_edges_in(p):
    member, source_x, source_y = choose(p.k, p.y, p.x), choose(p.k, p.x, p.y), choose(p.k, p.x, p.y)
    own = p.on_diagonal * same(p.k, member // 2)
    return [(p.in_relay * (1 - own), p.at(k=member // 2, x=source_x, y=source_y))]


def edges_in(p):
    source = choose(p.k, p.row, p.at(zh=p.zl)[0]), choose(p.k, p.at(zl=p.zh)[1], p.c)
    found = [(1 - p.in_relay, source)]
    for n in range(4):
        step, member = maker_of(p.c, 2 * n)
        step1, member1 = maker_of(p.c, 2 * n + 1)
        step, member = choose(p.k, step1, step), choose(p.k, member1, member)
        stays, own = same(step, 0), same(member, p.x)
        core = choose(stays, 0, choose(own, 0, p.k))
        found.append((1 - stays * own * (1 - p.k), (2 * (4 * p.zh + member) + core, p.c + own * step)))
        step, member = maker_of(p.R, n)
        step1, member1 = maker_of(p.R, 4 + n)
        step, member = choose(p.k, step1, step), choose(p.k, member1, member)
        stays, own = same(step, 0), same(member, p.y)
        core = choose(stays, 1, choose(own, 1, p.k))
        found.append((1 - stays * own * p.k, (2 * (p.R + own * step) + core, 4 * p.zl + member)))
    forward = 1 - p.k
    here = choose(forward, 1 - same(p.R, 0), 1 - same(p.R, GROUPS - 1))
    edge = same(p.x, choose(forward, 0, 3))
    source_row = (2 * (p.R + 1 - 2 * forward) + 1 - p.k + 32) % 32
    source_zh = source_row // 8
    for q in range(4):
        row = choose(edge, 8 * source_zh + 2 * q + 1 - p.k, source_row)
        found.append((here, (row, p.c)))
    relay, _, start = relay_role(p)
    found.append((relay, start))
    found.append((1, p.at(k=1 - p.k)))
    for side, cond, _, source in side_relay(p):
        found.append((cond, source))
        own_y = 0 if side else 3
        exists, crosses = 1 - same(p.c, GROUPS - 1 if side else 0), same(p.y, 3 - own_y)
        for q in range(4):
            col = choose(crosses, p.at(y=q, zl=(p.zl + (1 if side else 3)) % 4)[1], p.c - 1 + 2 * side)
            found.append((exists, (p.row, col)))
    return found


def here():
    return Place(lax.axis_index("row"), lax.axis_index("col"))


def when(cond, action):
    if isinstance(cond, int):
        if cond:
            action()
    else:
        pl.when(cond == 1)(action)


class Sends:
    def __init__(self, sems):
        self.sems, self.pending = sems, []

    def start(self, cond, source, target, recv_sem, device):
        index = len(self.pending)

        def make():
            return pltpu.make_async_remote_copy(
                src_ref=source,
                dst_ref=target,
                send_sem=self.sems.at[index],
                recv_sem=recv_sem,
                device_id=device,
                device_id_type=MESH,
            )

        self.pending.append((cond, make))
        when(cond, lambda: make().start())

    def finish(self):
        for cond, make in self.pending:
            when(cond, lambda make=make: make().wait_send())


def arrived(ref, sem, cond=1):
    when(cond, lambda: pltpu.make_async_copy(ref, ref, sem).wait())


def greet(edges_in, edges_out):
    barrier = pltpu.get_barrier_semaphore()
    for cond, device in edges_in:
        when(
            cond,
            lambda device=device: pl.semaphore_signal(barrier, inc=1, device_id=device, device_id_type=MESH),
        )
    count = sum(cond for cond, _ in edges_out)
    pl.when(count > 0)(lambda: pl.semaphore_wait(barrier, count))


def first_kernel(m_ref, out_ref, square, folded, received, load_sem, send_sem, receive_sem):
    p = here()
    loads = []
    for j in range(2):
        column = pl.multiple_of(p.k * ROWS + j * PAIR, PAIR)
        loads.append(
            pltpu.make_async_copy(
                m_ref.at[pl.ds(j * PAIR, PAIR), pl.ds(column, PAIR)], square.at[j], load_sem.at[j]
            )
        )
        when(p.on_diagonal, loads[j].start)

    def fold_both():
        for j in range(2):
            loads[j].wait()
            folded[j] = fold(square[j])

    when(p.on_diagonal, fold_both)
    greet(first_edges_in(p), first_edges_out(p))
    sends = Sends(send_sem)
    for j, _, own, cond, device in scatter_out(p):
        sends.start(cond, folded.at[j], received, receive_sem.at[0], device)
        when(own, pltpu.make_async_copy(folded.at[j], received, receive_sem.at[0]).start)

    def keep():
        pltpu.make_async_copy(received, received, receive_sem.at[0]).wait()
        out_ref[...] = received[...]

    when(p.in_relay, keep)
    when(1 - p.in_relay, lambda: out_ref.__setitem__(..., jnp.zeros((FOLD, BLK), F32)))
    sends.finish()


def travel_kernel(
    m_ref, first_ref, left_ref, right_ref, outer_ref, inner_ref, jc_ref, jr_ref,
    solver_in, out_c, out_r, relay, side_pass,
    send_sem, solver_sem, jc_sem, jr_sem, side_sem, outer_sem, outer_side_sem, inner_sem, relay_sem, side_pass_sem,
):
    p = here()
    greet(edges_in(p), edges_out(p))
    sends = Sends(send_sem)
    mate = p.at(k=1 - p.k)
    before, after = (p.row, p.c - 1), (p.row, p.c + 1)
    has_before, has_after = 1 - same(p.c, 0), 1 - same(p.c, GROUPS - 1)
    low = pl.multiple_of(p.k * PAIR, PAIR)
    other = pl.multiple_of((1 - p.k) * PAIR, PAIR)

    for cond, device in cross_out(p):
        sends.start(cond, first_ref, solver_in, solver_sem.at[0], device)

    sides = (left_ref, right_ref)
    for side, q, relayed, direct, device in side_out(p):
        part = m_ref.at[pl.ds(q * BLK, BLK), pl.ds(0 if side else COLS - PAIR, PAIR)]
        if not isinstance(relayed, int):
            sends.start(relayed, part, side_pass.at[side], side_pass_sem.at[side], device)
        sends.start(direct, part, sides[side].at[pl.ds(q * BLK, BLK)], side_sem.at[side, q], device)
    sends.start(1, m_ref.at[pl.ds(other, PAIR)], inner_ref.at[:, pl.ds(PAIR, COLS)], inner_sem.at[0], mate)
    for q, relayed, direct, device in outer_out(p):
        part = m_ref.at[pl.ds(low, PAIR), pl.ds(q * PAIR, PAIR)]
        sends.start(relayed, part, relay, relay_sem.at[0], device)
        sends.start(direct, part, outer_ref.at[:, pl.ds(PAIR + q * PAIR, PAIR)], outer_sem.at[q], device)

    for side, cond, device, _ in side_relay(p):
        arrived(side_pass.at[side], side_pass_sem.at[side], cond)
        part = pl.ds(pl.multiple_of(p.y * BLK, BLK), BLK)
        sends.start(cond, side_pass.at[side], sides[side].at[part], side_sem.at[side, p.y], device)

    arrived(solver_in, solver_sem.at[0], 1 - p.in_relay)
    relaying, relay_to, _ = relay_role(p)
    arrived(relay, relay_sem.at[0], relaying)
    sends.start(
        relaying, relay, outer_ref.at[:, pl.ds(pl.multiple_of(PAIR + p.x * PAIR, PAIR), PAIR)], outer_sem.at[p.x], relay_to
    )
    rotation = pair_rotation(unfold(jnp.where(p.in_relay == 1, first_ref[...], solver_in[...])))

    def keep_columns():
        for half in range(2):
            out_c[half] = rotation[:, half * BLK : (half + 1) * BLK]

    def keep_rows():
        flipped = rotation.T
        for half in range(2):
            out_r[half] = flipped[half * BLK : (half + 1) * BLK]

    when(1 - p.k, keep_columns)
    when(p.k, keep_rows)
    for kind, half, own, cond, device, slot in spread_out(p):
        source, target, sem = (out_c, jc_ref, jc_sem) if kind == "col" else (out_r, jr_ref, jr_sem)
        sends.start(cond, source.at[half], target.at[slot], sem.at[slot], device)
        if not isinstance(own, int):
            when(own, pltpu.make_async_copy(source.at[half], target.at[slot], sem.at[slot]).start)

    has_outer = choose(p.k, 1 - same(p.R, GROUPS - 1), 1 - same(p.R, 0))
    sends_on = choose(p.k, 1 - same(p.x, 3), 1 - same(p.x, 0))
    (_, _, _, next_device), *_ = outer_out(p)
    ends = (pl.ds(0, PAIR), pl.ds(PAIR + COLS, PAIR))
    for side, exists, edge_y in ((0, has_before, 0), (1, has_after, 3)):
        for q in range(4):
            arrived(sides[side].at[pl.ds(q * BLK, BLK)], side_sem.at[side, q], exists)
        sends.start(
            exists, sides[side].at[pl.ds(other, PAIR)], inner_ref.at[:, ends[side]], inner_sem.at[1 + side], mate
        )
        sends.start(
            sends_on * exists * same(p.y, edge_y), sides[side].at[pl.ds(low, PAIR)], outer_ref.at[:, ends[side]],
            outer_side_sem.at[side], next_device,
        )

    def outer_corners(cond):
        for q in range(4):
            arrived(outer_ref.at[:, pl.ds(PAIR + q * PAIR, PAIR)], outer_sem.at[q], cond * has_outer)
            if q == 0:
                sends.start(
                    cond * has_outer * has_before * (1 - sends_on * same(p.y, 0)), outer_ref.at[:, pl.ds(PAIR, PAIR)],
                    outer_ref.at[:, ends[1]], outer_side_sem.at[1], before,
                )
        sends.start(
            cond * has_outer * has_after * (1 - sends_on * same(p.y, 3)), outer_ref.at[:, pl.ds(COLS, PAIR)],
            outer_ref.at[:, ends[0]], outer_side_sem.at[0], after,
        )

    outer_corners(sends_on)
    (_, hub, _, _), (_, hub_r, _, _) = hub_out(p)
    for kind, cond, slot, devices in hub_out(p):
        target, sem = (jc_ref, jc_sem) if kind == "col" else (jr_ref, jr_sem)
        arrived(target.at[slot], sem.at[slot], cond)
        for device in devices:
            sends.start(cond, target.at[slot], target.at[slot], sem.at[slot], device)

    outer_corners(1 - sends_on)

    for n in (1, 2, 3, 0):
        slot = choose(p.k, (1, 3, 5, 7)[n - 1], 2 * n)
        arrived(jc_ref.at[slot], jc_sem.at[slot], 1 - hub * same(slot, 7 * p.k))
        sends.start(1, jc_ref.at[slot], jc_ref.at[slot], jc_sem.at[slot], mate)
    for n in range(4):
        arrived(jc_ref.at[2 * n + 1 - p.k], jc_sem.at[2 * n + 1 - p.k])
        arrived(jr_ref.at[n], jr_sem.at[n], 1 - hub_r * same(n, 3 * p.k))

    arrived(inner_ref.at[:, pl.ds(PAIR, COLS)], inner_sem.at[0])
    arrived(inner_ref.at[:, pl.ds(0, PAIR)], inner_sem.at[1], has_before)
    arrived(inner_ref.at[:, pl.ds(PAIR + COLS, PAIR)], inner_sem.at[2], has_after)
    arrived(outer_ref.at[:, pl.ds(0, PAIR)], outer_side_sem.at[0], has_outer * has_before)
    arrived(outer_ref.at[:, pl.ds(PAIR + COLS, PAIR)], outer_side_sem.at[1], has_outer * has_after)
    sends.finish()


MIB = 1024 * 1024


def first(matrix):
    return pl.pallas_call(
        first_kernel,
        out_shape=pltpu.VMEM((FOLD, BLK), F32),
        in_specs=[pl.BlockSpec(memory_space=pltpu.HBM)],
        out_specs=pl.BlockSpec(memory_space=pltpu.VMEM),
        scratch_shapes=[
            pltpu.VMEM((2, PAIR, PAIR), F32),
            pltpu.VMEM((2, FOLD, BLK), F32),
            pltpu.VMEM((FOLD, BLK), F32),
            pltpu.SemaphoreType.DMA((2,)),
            pltpu.SemaphoreType.DMA((4,)),
            pltpu.SemaphoreType.DMA((1,)),
        ],
        compiler_params=pltpu.CompilerParams(collective_id=0, has_side_effects=True, vmem_limit_bytes=62 * MIB),
        cost_estimate=pl.CostEstimate(flops=10**6, bytes_accessed=10**6, transcendentals=0),
        name="first",
    )(matrix)


def travel(matrix, folded):
    any_spec = pl.BlockSpec(memory_space=pl.ANY)
    shapes = [(ROWS, PAIR), (ROWS, PAIR), (PAIR, WIDE), (PAIR, WIDE), (8, PAIR, BLK), (4, BLK, PAIR)]
    return pl.pallas_call(
        travel_kernel,
        out_shape=[pltpu.VMEM(shape, F32) for shape in shapes],
        in_specs=[pl.BlockSpec(memory_space=pltpu.HBM), pl.BlockSpec(memory_space=pltpu.VMEM)],
        out_specs=[any_spec] * len(shapes),
        scratch_shapes=[
            pltpu.VMEM((FOLD, BLK), F32),
            pltpu.VMEM((2, PAIR, BLK), F32),
            pltpu.VMEM((2, BLK, PAIR), F32),
            pltpu.VMEM((PAIR, PAIR), F32),
            pltpu.VMEM((2, BLK, PAIR), F32),
            pltpu.SemaphoreType.DMA((112,)),
            pltpu.SemaphoreType.DMA((1,)),
            pltpu.SemaphoreType.DMA((8,)),
            pltpu.SemaphoreType.DMA((4,)),
            pltpu.SemaphoreType.DMA((2, 4)),
            pltpu.SemaphoreType.DMA((4,)),
            pltpu.SemaphoreType.DMA((2,)),
            pltpu.SemaphoreType.DMA((3,)),
            pltpu.SemaphoreType.DMA((1,)),
            pltpu.SemaphoreType.DMA((2,)),
        ],
        compiler_params=pltpu.CompilerParams(collective_id=1, has_side_effects=True, vmem_limit_bytes=32 * MIB),
        cost_estimate=pl.CostEstimate(flops=10**9, bytes_accessed=10**7, transcendentals=0),
        name="travel",
    )(matrix, folded)


SLOTS = (((0,), 0), ((1, 4), 2), ((2,), 1), ((3, 6), 3), ((5,), 4), ((7,), 5))


def apply_kernel(
    m_ref, left_ref, right_ref, outer_ref, inner_ref, jc, jr, o_ref, own, half_high, half_low, result, own_sem, out_sem,
):
    p = here()
    first_row, last_row = same(p.row, 0), same(p.row, 2 * GROUPS - 1)
    loads = []
    for pair in (1, 0):
        rows = pl.ds(pair * PAIR, PAIR)
        loads.append(pltpu.make_async_copy(m_ref.at[rows], own.at[rows], own_sem.at[pair]))
        loads[-1].start()
    low, middle, high = pl.ds(0, PAIR), pl.ds(PAIR, COLS), pl.ds(PAIR + COLS, PAIR)

    def turn(s, parts):
        high_j, low_j = split(jr[s])
        stacked = jnp.concatenate([high_j, low_j], axis=0)
        for columns, part in parts:
            high_m, low_m = split(part())
            both = jnp.dot(stacked, high_m, preferred_element_type=F32)
            turned = both[:BLK] + both[BLK:] + jnp.dot(high_j, low_m, preferred_element_type=F32)
            turned_high, turned_low = split(turned)
            half_high[s * BLK : (s + 1) * BLK, columns] = turned_high
            half_low[s * BLK : (s + 1) * BLK, columns] = turned_low

    def own_rows(s, pair):
        rows = pl.ds(pair * PAIR, PAIR)
        turn(s, ((middle, lambda: own[rows]), (low, lambda: left_ref[rows]), (high, lambda: right_ref[rows])))

    def sent_rows(s, ref):
        turn(s, ((middle, lambda: ref[:, middle]), (low, lambda: ref[:, low]), (high, lambda: ref[:, high])))

    when((1 - p.k) * (1 - first_row), lambda: sent_rows(0, outer_ref))
    when(p.k, lambda: sent_rows(0, inner_ref))
    when(p.k * (1 - last_row), lambda: sent_rows(3, outer_ref))
    when(1 - p.k, lambda: sent_rows(3, inner_ref))
    for load in loads:
        load.wait()
    own_rows(1, 1)
    own_rows(2, 0)
    when(first_row, lambda: own_rows(0, 0))
    when(last_row, lambda: own_rows(3, 1))

    def repeat(target, source):
        half_high[:, target] = half_high[:, source]
        half_low[:, target] = half_low[:, source]

    when(same(p.c, 0), lambda: repeat(low, pl.ds(PAIR, PAIR)))
    when(same(p.c, GROUPS - 1), lambda: repeat(high, pl.ds(COLS, PAIR)))
    stores = []
    for slots, panel in SLOTS:
        columns = pl.ds(panel * PAIR, PAIR)
        if len(slots) == 1:
            high_j, low_j = split(jc[slots[0]])
            both = jnp.dot(
                half_high[:, columns], jnp.concatenate([high_j, low_j], axis=1), preferred_element_type=F32
            )
            turned = both[:, :BLK] + both[:, BLK:] + jnp.dot(half_low[:, columns], high_j, preferred_element_type=F32)
        else:
            rotation = jnp.concatenate([jc[slots[0]], jc[slots[1]]], axis=1)
            turned = product((half_high[:, columns], half_low[:, columns]), split(rotation))
        for n, slot in enumerate(slots):
            result[slot] = turned[:, n * BLK : (n + 1) * BLK]
            store = pltpu.make_async_copy(result.at[slot], o_ref.at[:, pl.ds(slot * BLK, BLK)], out_sem.at[slot])
            store.start()
            stores.append(store)
    for store in stores:
        store.wait()


def apply(matrix, parts):
    hbm = pl.BlockSpec(memory_space=pltpu.HBM)
    vmem = pl.BlockSpec(memory_space=pltpu.VMEM)
    return pl.pallas_call(
        apply_kernel,
        out_shape=jax.ShapeDtypeStruct((ROWS, COLS), F32),
        in_specs=[hbm] + [vmem] * 6,
        out_specs=pl.BlockSpec(memory_space=pl.ANY),
        scratch_shapes=[
            pltpu.VMEM((ROWS, COLS), F32),
            pltpu.VMEM((ROWS, WIDE), BF16),
            pltpu.VMEM((ROWS, WIDE), BF16),
            pltpu.VMEM((8, ROWS, BLK), F32),
            pltpu.SemaphoreType.DMA((2,)),
            pltpu.SemaphoreType.DMA((8,)),
        ],
        compiler_params=pltpu.CompilerParams(vmem_limit_bytes=48 * MIB),
        cost_estimate=pl.CostEstimate(flops=2 * 10**9, bytes_accessed=10**7, transcendentals=0),
        name="apply",
    )(matrix, *parts)


def local(matrix):
    matrix = pltpu.with_memory_space_constraint(matrix, pltpu.HBM)
    return apply(matrix, travel(matrix, first(matrix)))


def solution(mesh):
    spec = P("row", "col")
    return jax.shard_map(local, mesh=mesh, in_specs=(spec,), out_specs=spec, check_vma=False)
```
